256 devices in a mesh: pair: 2 (over x_hi), tp: 8 (over y, x_lo), dp: 16 (over z, core).
Axes of the slice: x: 4 (x_hi: 2, x_lo: 2; x = x_hi * 2 + x_lo), y: 4, z: 8, core: 2. Of those that a mesh axis runs over, the one named last changes fastest.
Arguments:
- x_prompt: bfloat16 [16, 512, 4608], P('dp', ('pair', 'tp')), may hold values from -6 to 6
- x_comp: bfloat16 [16, 2, 128, 4608], P('dp', 'pair', 'tp'), may hold values from -6 to 6
- up_prompt: bfloat16 [16, 512, 4608], P('dp', ('pair', 'tp')), may hold values from -0.4 to 0.4
- up_comp: bfloat16 [16, 2, 128, 4608], P('dp', 'pair', 'tp'), may hold values from -0.4 to 0.4
- w_q: bfloat16 [4608, 2048], P(None, 'tp'), may hold values from -0.14731391 to 0.14731391
- key_projection: bfloat16 [4608, 1024], P(None, 'tp'), may hold values from -0.09375 to 0.09375
- value_projection: bfloat16 [4608, 1024], P(None, 'tp'), may hold values from -0.09375 to 0.09375
- w_o: bfloat16 [2048, 4608], P('tp'), may hold values from -0.15467961 to 0.15467961
- pre_gain: float32 [4608], replicated, may hold values from 0.5 to 1.5
- post_gain: float32 [4608], replicated, may hold values from 0.25 to 1.75
- dpo_weight: float32 [16], P('dp'), may hold values from 0.1 to 1
- prompt_len: int32 [16], P('dp'), may hold values from 257 to 512, as said below
- comp_len: int32 [16, 2], P('dp', 'pair'), may hold values from 32 to 128, as said below
- loss_mask: int32 [16, 2, 128], P('dp', 'pair'), may hold values 0 or 1
Outputs:
- out_prompt: bfloat16 [16, 512, 4608], P('dp', ('pair', 'tp'))
- out_comp: bfloat16 [16, 2, 128, 4608], P('dp', 'pair', 'tp')
- grad_wq: float32 [4608, 2048], P(('pair', 'dp'), 'tp')
- grad_wk: float32 [4608, 1024], P(('pair', 'dp'), 'tp')
- grad_wv: float32 [4608, 1024], P(('pair', 'dp'), 'tp')
- grad_wo: float32 [2048, 4608], P('tp', ('pair', 'dp'))
The draws below stay inside these ranges and needn't reach their ends.
Inputs may be any that keep to these rules, and one draw needn't show every extreme that they name: Tokens past prompt_len are padding; some pair's prompt has all 512 tokens real. Tokens past comp_len are padding; some completion has all 128 tokens real.
All inputs are finite; a program needn't handle non-finite values. No bound on the sum of `loss_mask` on one device may be relied on, other than what follows from the above.
Results may differ from the reference program's by a relative error of at most 0.029.
Values may be sent and summed in bfloat16 or wider, within the bound.
A program may use at most 128 MiB of HBM per device.

```python
import math
import jax
import jax.numpy as jnp
from jax import lax

MODEL_WIDTH = 4608
HEAD_SIZE = 128
HQ = 16
KEY_VALUE_HEADS = 8
PROMPT = 512
CL = 128
PAIRS = 16
N_TP = 8


def shared_structure(key):
    shared_key = jax.random.fold_in(key, 101)
    direction_key, pairing_key = jax.random.split(shared_key)
    direction = jnp.clip(jax.random.normal(direction_key, (MODEL_WIDTH,), jnp.float32), -2.0, 2.0)
    pairing = jax.random.permutation(pairing_key, 2 * PAIRS).astype(jnp.int32)
    block_width = MODEL_WIDTH // (2 * PAIRS)
    column_block = jnp.arange(MODEL_WIDTH, dtype=jnp.int32) // block_width
    spike_gain = jnp.where(column_block[None, :] == pairing[:, None], 3.0, 1.0).astype(jnp.float32)
    return (direction, spike_gain)


def draw_prompt_len(key, part):
    key = jax.random.fold_in(key, 11)
    lengths_key, picked_key = jax.random.split(key)
    lengths = jax.random.randint(lengths_key, (PAIRS,), PROMPT // 2 + 1, PROMPT + 1, dtype=jnp.int32)
    picked = jax.random.randint(picked_key, (), 0, PAIRS, dtype=jnp.int32)
    return jnp.where(jnp.arange(PAIRS, dtype=jnp.int32) == picked, PROMPT, lengths).astype(jnp.int32)


def draw_comp_len(key, part):
    key = jax.random.fold_in(key, 23)
    lengths_key, picked_key = jax.random.split(key)
    lengths = jax.random.randint(lengths_key, (PAIRS * 2,), CL // 4, CL + 1, dtype=jnp.int32)
    picked = jax.random.randint(picked_key, (), 0, PAIRS * 2, dtype=jnp.int32)
    filled = jnp.where(jnp.arange(PAIRS * 2, dtype=jnp.int32) == picked, CL, lengths)
    return filled.reshape(PAIRS, 2).astype(jnp.int32)


def draw_w_q(key, part):
    key = jax.random.fold_in(key, 37)
    noise_key, gain_key = jax.random.split(key)
    noise = jnp.clip(jax.random.normal(noise_key, (MODEL_WIDTH, HQ * HEAD_SIZE), jnp.float32), -2.5, 2.5)
    head_gain = 4.0 ** jax.random.uniform(gain_key, (HQ,), jnp.float32)
    column_gain = jnp.repeat(head_gain, HEAD_SIZE)
    return (noise * column_gain[None, :] * MODEL_WIDTH ** (-0.5)).astype(jnp.bfloat16)


def draw_w_o(key, part):
    direction = shared_structure(key)[0]
    key = jax.random.fold_in(key, 53)
    noise_key, mixing_key = jax.random.split(key)
    noise_values = jnp.clip(jax.random.normal(noise_key, (HQ * HEAD_SIZE, MODEL_WIDTH), jnp.float32), -3.0, 3.0)
    mixing = jnp.clip(jax.random.normal(mixing_key, (HQ * HEAD_SIZE,), jnp.float32), -2.0, 2.0)
    values = (noise_values + mixing[:, None] * direction[None, :]) * (HQ * HEAD_SIZE) ** (-0.5)
    return values.astype(jnp.bfloat16)


def draw_up_prompt(key, part):
    direction, spike_gain = shared_structure(key)
    key = jax.random.fold_in(key, 41)
    noise_key, coef_key = jax.random.split(key)
    noise_values = jnp.clip(jax.random.normal(noise_key, (PAIRS, PROMPT, MODEL_WIDTH), jnp.float32), -2.5, 2.5)
    row_coef = jnp.clip(jax.random.normal(coef_key, (PAIRS, PROMPT, 1), jnp.float32), -2.0, 2.0)
    side_of_row = jnp.arange(PROMPT, dtype=jnp.int32) // (PROMPT // 2)
    slot_index = 2 * jnp.arange(PAIRS, dtype=jnp.int32)[:, None] + side_of_row[None, :]
    row_gains = spike_gain[slot_index]
    values = 0.05 * (noise_values * row_gains + row_coef * direction[None, None, :])
    return jnp.clip(values, -0.3984375, 0.3984375).astype(jnp.bfloat16)


def draw_up_comp(key, part):
    direction, spike_gain = shared_structure(key)
    key = jax.random.fold_in(key, 47)
    noise_key, coef_key = jax.random.split(key)
    noise_values = jnp.clip(jax.random.normal(noise_key, (PAIRS, 2, CL, MODEL_WIDTH), jnp.float32), -2.5, 2.5)
    row_coef = jnp.clip(jax.random.normal(coef_key, (PAIRS, 2, CL, 1), jnp.float32), -2.0, 2.0)
    slot_index = 2 * jnp.arange(PAIRS, dtype=jnp.int32)[:, None] + jnp.arange(2, dtype=jnp.int32)[None, :]
    row_gains = spike_gain[slot_index][:, :, None, :]
    values = 0.05 * (noise_values * row_gains + row_coef * direction[None, None, None, :])
    return jnp.clip(values, -0.3984375, 0.3984375).astype(jnp.bfloat16)


def touch_ends(entries, rng, low, high):
    longest = entries.shape.index(max(entries.shape))
    spots = []
    for shift in (0, 1):
        where = [jax.random.randint(jax.random.fold_in(rng, axis), (), 0, length) for axis, length in enumerate(entries.shape)]
        where[longest] = (where[longest] + shift) % entries.shape[longest]
        spots.append(tuple(where))
    return entries.at[spots[0]].set(low).at[spots[1]].set(high)


def levels(stream_key, shape, cuts, least, high):
    def one(axis_at, shards_of):
        heights = jax.random.uniform(jax.random.fold_in(jax.random.fold_in(stream_key, 6), axis_at), (shards_of,), jnp.float32, least / len(cuts), high / len(cuts))
        return jnp.repeat(jnp.exp(heights), shape[axis_at] // shards_of).reshape((-1,) + (1,) * (len(shape) - axis_at - 1))

    level = one(*cuts[0])
    for cut in cuts[1:]:
        level = level * one(*cut)
    return level


def normal_values(own_key, extent, spread, most, cuts=(), kind=jnp.bfloat16):
    array = jax.random.normal(own_key, extent, jnp.float32) * spread
    if len(cuts) > 0:
        array = levels(own_key, extent, cuts, -0.22, 0.18) * array
    return jnp.clip(array, min=-most, max=most).astype(kind)


def setup_inputs(seed: int = 0) -> dict:
    splits = jax.random.split(jax.random.key(seed), 15)
    x_prompt = normal_values(splits[0], (PAIRS, PROMPT, MODEL_WIDTH), 1.0, 6.0, ((0, 16), (1, 16)))
    x_comp = normal_values(splits[1], (PAIRS, 2, CL, MODEL_WIDTH), 1.0, 6.0, ((0, 16), (1, 2), (2, 8)))
    up_prompt = draw_up_prompt(jax.random.fold_in(splits[14], 71), 0)
    up_comp = draw_up_comp(jax.random.fold_in(splits[14], 71), 0)
    w_q = draw_w_q(jax.random.fold_in(splits[14], 71), 0)
    key_projection = normal_values(splits[5], (MODEL_WIDTH, KEY_VALUE_HEADS * HEAD_SIZE), MODEL_WIDTH ** -0.5, 0.09375, ((1, 8),))
    value_projection = normal_values(splits[6], (MODEL_WIDTH, KEY_VALUE_HEADS * HEAD_SIZE), MODEL_WIDTH ** -0.5, 0.09375, ((1, 8),))
    w_o = draw_w_o(jax.random.fold_in(splits[14], 71), 0)
    pre_gain = jnp.clip(1.0 + 0.1 * jax.random.normal(splits[8], (MODEL_WIDTH,), jnp.float32), 0.5, 1.5)
    post_gain = jnp.clip(1.0 + 0.15 * jax.random.normal(splits[9], (MODEL_WIDTH,), jnp.float32), 0.25, 1.75)
    dpo_weight = jnp.clip(jnp.exp(math.log(1.0) - 2.3025851 * jax.random.uniform(splits[10], (PAIRS,), jnp.float32) ** levels(splits[10], (PAIRS,), ((0, 16),), -0.2, 0.2)), 0.1, 1.0)
    prompt_len = draw_prompt_len(jax.random.fold_in(splits[14], 71), 0)
    comp_len = draw_comp_len(jax.random.fold_in(splits[14], 71), 0)
    loss_mask = touch_ends((jax.random.randint(splits[13], (PAIRS, 2, CL), 0, 4) < 3).astype(jnp.int32), jax.random.fold_in(splits[13], 1), 0, 1)
    return dict(x_prompt=x_prompt, x_comp=x_comp, up_prompt=up_prompt, up_comp=up_comp, w_q=w_q, key_projection=key_projection, value_projection=value_projection, w_o=w_o, pre_gain=pre_gain, post_gain=post_gain, dpo_weight=dpo_weight, prompt_len=prompt_len, comp_len=comp_len, loss_mask=loss_mask)


softcap = 50.0
query_scale = 144.0 ** (-0.5)
rope_base = 10000.0
norm_eps = 1e-06

def inverse_norm(values):
    return lax.rsqrt(lax.optimization_barrier(jnp.mean(values * values, axis=-1, keepdims=True)) + norm_eps)

def rotate(values, positions, rotation_sign):
    row_count = values.shape[0]
    grouped = values.reshape(row_count, -1, HEAD_SIZE)
    half_head = HEAD_SIZE // 2
    frequencies = rope_base ** (-2.0 * jnp.arange(half_head, dtype=jnp.float32) / HEAD_SIZE)
    angles = positions.astype(jnp.float32)[:, None] * frequencies[None, :]
    cosine = jnp.cos(angles)[:, None, :]
    sine_part = rotation_sign * jnp.sin(angles)[:, None, :]
    lower_half = grouped[..., :half_head]
    upper_half = grouped[..., half_head:]
    turned = jnp.concatenate([lower_half * cosine - upper_half * sine_part, upper_half * cosine + lower_half * sine_part], axis=-1)
    return turned.reshape(row_count, -1)

def rounded(values):
    return lax.optimization_barrier(values.astype(jnp.bfloat16)).astype(jnp.float32)

def attend(queries, key_rows, value_rows, allowed):
    row_count = queries.shape[0]
    kv_heads = key_rows.shape[1] // HEAD_SIZE
    query_groups = queries.astype(jnp.float32).reshape(row_count, kv_heads, -1, HEAD_SIZE)
    key_groups = key_rows.astype(jnp.float32).reshape(-1, kv_heads, HEAD_SIZE)
    value_groups = value_rows.astype(jnp.float32).reshape(-1, kv_heads, HEAD_SIZE)
    scores = jnp.einsum('rgjd,kgd->gjrk', query_groups, key_groups)
    bounded = jnp.tanh(scores / softcap)
    raw_weights = jnp.where(allowed, jnp.exp(softcap * bounded), 0.0)
    probabilities = raw_weights / lax.optimization_barrier(jnp.sum(raw_weights, axis=-1, keepdims=True))
    weights = rounded(probabilities)
    attended = jnp.einsum('gjrk,kgd->rgjd', weights, value_groups)
    return (attended.reshape(row_count, -1).astype(jnp.bfloat16), probabilities, bounded)

def attend_back(grad_attended, queries, key_rows, value_rows, probabilities, bounded):
    row_count = queries.shape[0]
    kv_heads = key_rows.shape[1] // HEAD_SIZE
    query_groups = queries.astype(jnp.float32).reshape(row_count, kv_heads, -1, HEAD_SIZE)
    key_groups = key_rows.astype(jnp.float32).reshape(-1, kv_heads, HEAD_SIZE)
    value_groups = value_rows.astype(jnp.float32).reshape(-1, kv_heads, HEAD_SIZE)
    grad_groups = grad_attended.astype(jnp.float32).reshape(row_count, kv_heads, -1, HEAD_SIZE)
    weights = rounded(probabilities)
    grad_probs = jnp.einsum('rgjd,kgd->gjrk', grad_groups, value_groups)
    value_gradients = jnp.einsum('gjrk,rgjd->kgd', weights, grad_groups)
    centered = probabilities * (grad_probs - lax.optimization_barrier(jnp.sum(probabilities * grad_probs, axis=-1, keepdims=True)))
    grad_scores = rounded(centered * (1.0 - bounded * bounded))
    grad_queries = jnp.einsum('gjrk,kgd->rgjd', grad_scores, key_groups).reshape(row_count, -1)
    grad_keys = jnp.einsum('gjrk,rgjd->kgd', grad_scores, query_groups).reshape(-1, kv_heads * HEAD_SIZE)
    return (grad_queries, grad_keys, value_gradients.reshape(-1, kv_heads * HEAD_SIZE))

def reference(x_prompt, x_comp, up_prompt, up_comp, w_q, key_projection, value_projection, w_o, pre_gain, post_gain, dpo_weight, prompt_len, comp_len, loss_mask):
    half_rows = PROMPT // 2
    group_cols = HQ * HEAD_SIZE // N_TP
    q_cols = HQ * HEAD_SIZE
    key_value_columns = KEY_VALUE_HEADS * HEAD_SIZE

    def project(normed, positions):
        queries = (rotate(jnp.dot(normed, w_q, preferred_element_type=jnp.float32), positions, 1.0) * query_scale).astype(jnp.bfloat16)
        key_rows = rotate(jnp.dot(normed, key_projection, preferred_element_type=jnp.float32), positions, 1.0).astype(jnp.bfloat16)
        value_rows = jnp.dot(normed, value_projection, preferred_element_type=jnp.float32).astype(jnp.bfloat16)
        return (queries, key_rows, value_rows)

    def one_pair(carry, items):
        grad_in, grad_out = carry
        prompt_x, comp_x, prompt_up, comp_up, weight, length, comp_lengths, comp_keep = items
        prompt_pos = jnp.arange(PROMPT, dtype=jnp.int32)
        comp_index = jnp.arange(CL, dtype=jnp.int32)
        comp_pos = length + comp_index
        prompt_f = prompt_x.astype(jnp.float32)
        comp_f = comp_x.astype(jnp.float32)
        prompt_norm = (prompt_f * inverse_norm(prompt_f) * pre_gain).astype(jnp.bfloat16)
        comp_norm = (comp_f * inverse_norm(comp_f) * pre_gain).astype(jnp.bfloat16)
        prompt_q, prompt_k, prompt_v = project(prompt_norm, prompt_pos)
        columns = jnp.arange(PROMPT + CL, dtype=jnp.int32)
        col_prompt = columns < PROMPT
        comp_allowed = (col_prompt & (columns < length))[None, :] | (~col_prompt)[None, :] & (columns[None, :] - PROMPT <= comp_index[:, None])
        outs_prompt = []
        outs_comp = []
        saved = []
        key_grad_prompt = jnp.zeros((PROMPT, key_value_columns), jnp.float32)
        value_grad_prompt = jnp.zeros((PROMPT, key_value_columns), jnp.float32)
        for pair_side in range(2):
            lower_row = pair_side * half_rows
            comp_q, comp_k, comp_v = project(comp_norm[pair_side], comp_pos)
            prompt_index = lower_row + jnp.arange(half_rows, dtype=jnp.int32)
            prompt_allowed = col_prompt[None, :] & (columns[None, :] <= prompt_index[:, None])
            allowed = jnp.concatenate([prompt_allowed, comp_allowed], axis=0)
            queries = jnp.concatenate([prompt_q[lower_row:lower_row + half_rows], comp_q], axis=0)
            key_rows = jnp.concatenate([prompt_k, comp_k], axis=0)
            value_rows = jnp.concatenate([prompt_v, comp_v], axis=0)
            attended, probabilities, bounded = attend(queries, key_rows, value_rows, allowed)
            branch = jnp.zeros((half_rows + CL, MODEL_WIDTH), jnp.float32)
            for group in range(N_TP):
                term = jnp.dot(attended[:, group * group_cols:(group + 1) * group_cols], w_o[group * group_cols:(group + 1) * group_cols], preferred_element_type=jnp.float32)
                branch = branch + rounded(term)
            own_x = jnp.concatenate([prompt_f[lower_row:lower_row + half_rows], comp_f[pair_side]], axis=0)
            post_scale = inverse_norm(branch)
            output_rows = (own_x + branch * post_scale * post_gain).astype(jnp.bfloat16)
            outs_prompt.append(output_rows[:half_rows])
            outs_comp.append(output_rows[half_rows:])
            prompt_factor = (prompt_index < length).astype(jnp.float32)
            comp_factor = weight * (1.0 - 2.0 * pair_side) * comp_keep[pair_side].astype(jnp.float32) * (comp_index < comp_lengths[pair_side]).astype(jnp.float32)
            factor = jnp.concatenate([prompt_factor, comp_factor], axis=0)
            cotangent = jnp.concatenate([prompt_up[lower_row:lower_row + half_rows], comp_up[pair_side]], axis=0).astype(jnp.float32) * factor[:, None]
            scaled = cotangent * post_gain
            grad_branch = (post_scale * scaled - branch * post_scale ** 3 * lax.optimization_barrier(jnp.mean(branch * scaled, axis=-1, keepdims=True))).astype(jnp.bfloat16)
            grad_attended = jnp.dot(grad_branch, w_o.T, preferred_element_type=jnp.float32).astype(jnp.bfloat16)
            grad_queries, grad_keys, value_gradients = attend_back(grad_attended, queries, key_rows, value_rows, probabilities, bounded)
            key_grad_prompt = key_grad_prompt + grad_keys[:PROMPT]
            value_grad_prompt = value_grad_prompt + value_gradients[:PROMPT]
            saved.append((grad_queries, grad_keys[PROMPT:], value_gradients[PROMPT:], attended, grad_branch))
        for pair_side in range(2):
            lower_row = pair_side * half_rows
            grad_queries, comp_gk, comp_gv, attended, grad_branch = saved[pair_side]
            positions = jnp.concatenate([prompt_pos[lower_row:lower_row + half_rows], comp_pos], axis=0)
            side_keys = jnp.concatenate([key_grad_prompt[lower_row:lower_row + half_rows], comp_gk], axis=0)
            side_values = jnp.concatenate([value_grad_prompt[lower_row:lower_row + half_rows], comp_gv], axis=0)
            grad_proj = jnp.concatenate([(rotate(grad_queries, positions, -1.0) * query_scale).astype(jnp.bfloat16), rotate(side_keys, positions, -1.0).astype(jnp.bfloat16), side_values.astype(jnp.bfloat16)], axis=1)
            normed_rows = jnp.concatenate([prompt_norm[lower_row:lower_row + half_rows], comp_norm[pair_side]], axis=0)
            grad_in = grad_in + rounded(jnp.dot(normed_rows.T, grad_proj, preferred_element_type=jnp.float32))
            grad_out = grad_out + rounded(jnp.dot(attended.T, grad_branch, preferred_element_type=jnp.float32))
        out_p = jnp.concatenate(outs_prompt, axis=0)
        out_c = jnp.stack(outs_comp, axis=0)
        return ((grad_in, grad_out), (out_p, out_c))
    start = (jnp.zeros((MODEL_WIDTH, q_cols + 2 * key_value_columns), jnp.float32), jnp.zeros((q_cols, MODEL_WIDTH), jnp.float32))
    (grad_in, grad_out), (out_prompt, out_comp) = lax.scan(one_pair, start, (x_prompt, x_comp, up_prompt, up_comp, dpo_weight, prompt_len, comp_len, loss_mask))
    return (out_prompt, out_comp, grad_in[:, :q_cols], grad_in[:, q_cols:q_cols + key_value_columns], grad_in[:, q_cols + key_value_columns:], grad_out)
```

```python
import jax
import jax.numpy as jnp
from jax import lax
from jax.experimental import pallas as pl
from jax.experimental.pallas import tpu as pltpu
from jax.sharding import PartitionSpec as P

HEAD_SIZE = 128


softcap = 50.0
query_scale = 144.0 ** (-0.5)
rope_base = 10000.0
norm_eps = 1e-06


def from_partner(block, axis, distance):
    count = lax.axis_size(axis)
    route = []
    for low in range(count):
        high = low | 1 << distance
        if high != low and high < count:
            route += [(low, high), (high, low)]
    return lax.ppermute(block, axis, route)


def inverse_norm(values):
    return lax.rsqrt(jnp.mean(values * values, axis=-1, keepdims=True) + norm_eps)


def rotate(values, positions, rotation_sign):
    row_count = values.shape[0]
    grouped = values.reshape(row_count, -1, HEAD_SIZE)
    half_head = HEAD_SIZE // 2
    frequencies = rope_base ** (-2.0 * jnp.arange(half_head, dtype=jnp.float32) / HEAD_SIZE)
    angles = positions.astype(jnp.float32)[:, None] * frequencies[None, :]
    cosine = jnp.cos(angles)[:, None, :]
    sine_part = rotation_sign * jnp.sin(angles)[:, None, :]
    lower_half = grouped[..., :half_head]
    upper_half = grouped[..., half_head:]
    turned = jnp.concatenate(
        [
            lower_half * cosine - upper_half * sine_part,
            upper_half * cosine + lower_half * sine_part,
        ],
        axis=-1,
    )
    return turned.reshape(row_count, -1)


def attend(queries, key_rows, value_rows, allowed):
    row_count = queries.shape[0]
    kv_heads = key_rows.shape[1] // HEAD_SIZE
    query_groups = queries.reshape(row_count, kv_heads, -1, HEAD_SIZE)
    key_groups = key_rows.reshape(-1, kv_heads, HEAD_SIZE)
    value_groups = value_rows.reshape(-1, kv_heads, HEAD_SIZE)
    scores = jnp.einsum(
        "rgjd,kgd->gjrk", query_groups, key_groups, preferred_element_type=jnp.float32
    )
    bounded = jnp.tanh(scores / softcap)
    raw_weights = jnp.where(allowed, jnp.exp(softcap * bounded), 0.0)
    probabilities = raw_weights / jnp.sum(raw_weights, axis=-1, keepdims=True)
    weights = probabilities.astype(jnp.bfloat16)
    attended = jnp.einsum(
        "gjrk,kgd->rgjd", weights, value_groups, preferred_element_type=jnp.float32
    )
    return (attended.reshape(row_count, -1).astype(jnp.bfloat16), probabilities, bounded, weights)


def attend_back(grad_attended, queries, key_rows, value_rows, probabilities, bounded, weights):
    row_count = queries.shape[0]
    kv_heads = key_rows.shape[1] // HEAD_SIZE
    query_groups = queries.reshape(row_count, kv_heads, -1, HEAD_SIZE)
    key_groups = key_rows.reshape(-1, kv_heads, HEAD_SIZE)
    value_groups = value_rows.reshape(-1, kv_heads, HEAD_SIZE)
    grad_groups = grad_attended.reshape(row_count, kv_heads, -1, HEAD_SIZE)
    grad_probs = jnp.einsum(
        "rgjd,kgd->gjrk", grad_groups, value_groups, preferred_element_type=jnp.float32
    )
    value_gradients = jnp.einsum(
        "gjrk,rgjd->kgd", weights, grad_groups, preferred_element_type=jnp.float32
    )
    centered = probabilities * (
        grad_probs - jnp.sum(probabilities * grad_probs, axis=-1, keepdims=True)
    )
    grad_scores = (centered * (1.0 - bounded * bounded)).astype(jnp.bfloat16)
    grad_queries = jnp.einsum(
        "gjrk,kgd->rgjd", grad_scores, key_groups, preferred_element_type=jnp.float32
    ).reshape(row_count, -1)
    grad_keys = jnp.einsum(
        "gjrk,rgjd->kgd", grad_scores, query_groups, preferred_element_type=jnp.float32
    ).reshape(-1, kv_heads * HEAD_SIZE)
    return (grad_queries, grad_keys, value_gradients.reshape(-1, kv_heads * HEAD_SIZE))


def grad_of_branch(branch, up_rows, factor, post_gain):
    cotangent = up_rows.astype(jnp.float32) * factor[:, None]
    post_scale = inverse_norm(branch)
    scaled = cotangent * post_gain
    return (
        post_scale * scaled
        - branch * post_scale**3 * jnp.mean(branch * scaled, axis=-1, keepdims=True)
    ).astype(jnp.bfloat16)


MESH = pl.DeviceIdType.MESH
PIECE = 768
PLUS, MINUS, CROSS = 0, 1, 2
STEPS = 14
SENDS = (
    [((0, 0), k) for k in (3, 4, 5, 0, 1, 2)]
    + [((0, -1), k) for k in (3, 4, 5)]
    + [((1, 0), k) for k in (3, 4)]
    + [((1, -1), k) for k in (3, 4, 5)],
    [((0, 0), k) for k in (0, 1, 2, 3, 4, 5)]
    + [((0, 1), k) for k in (0, 1, 2)]
    + [((1, 0), k) for k in (0, 1)]
    + [((1, 1), k) for k in (0, 1, 2)],
    [((0, 0), k) for k in (0, 3, 1, 4, 2, 5)]
    + [
        ((0, 1), 2),
        ((0, -1), 5),
        ((0, 1), 3),
        ((0, -1), 0),
        ((0, 1), 4),
        ((0, -1), 1),
        ((0, 1), 5),
        ((0, -1), 2),
    ],
)


def seen_from(stream, owner):
    flip, shift = owner
    if stream == CROSS:
        return (1 - flip, shift % 4)
    return (flip, (shift + (1 if stream == MINUS else -1)) % 4)


ARRIVALS = tuple(
    [(seen_from(s, owner), piece) for owner, piece in SENDS[s]] for s in range(3)
)


def ready_step(stream, pos):
    (flip, shift), piece = SENDS[stream][pos]
    if (flip, shift) == (0, 0):
        return -1
    spots = [
        p
        for s in range(3)
        for p in range(STEPS)
        if ARRIVALS[s][p] == ((flip, shift % 4), piece)
    ]
    return spots[0]


def tp_rank_of(owner):
    me = lax.axis_index("tp")
    flip, shift = owner
    return lax.rem(me // 2 + shift % 4, 4) * 2 + lax.rem(me + flip, 2)


def stream_target(stream):
    return {"tp": tp_rank_of([(0, 1), (0, 3), (1, 0)][stream])}


def stream_source(stream):
    return {"tp": tp_rank_of([(0, 3), (0, 1), (1, 0)][stream])}


def tp_barrier():
    barrier = pltpu.get_barrier_semaphore()
    for stream in range(3):
        pl.semaphore_signal(
            barrier, inc=1, device_id=stream_target(stream), device_id_type=MESH
        )
    pl.semaphore_wait(barrier, 3)


def cols(piece):
    return pl.ds(piece * PIECE, PIECE)


class Gather:
    def __init__(self, buf, rows, send_sems, recv_sems, first_sem=0):
        self.buf, self.rows = buf, rows
        self.send_sems, self.recv_sems, self.first = send_sems, recv_sems, first_sem
        self.started = [0, 0, 0]

    def copy(self, stream, pos):
        owner, piece = SENDS[stream][pos]
        ref = self.buf.at[tp_rank_of(owner), self.rows, cols(piece)]
        sem = self.first + stream * STEPS + pos
        return pltpu.make_async_remote_copy(
            src_ref=ref,
            dst_ref=ref,
            send_sem=self.send_sems.at[sem],
            recv_sem=self.recv_sems.at[sem],
            device_id=stream_target(stream),
            device_id_type=MESH,
        )

    def arrival(self, stream, pos):
        owner, piece = ARRIVALS[stream][pos]
        ref = self.buf.at[tp_rank_of(owner), self.rows, cols(piece)]
        sem = self.first + stream * STEPS + pos
        return pltpu.make_async_remote_copy(
            src_ref=ref,
            dst_ref=ref,
            send_sem=self.send_sems.at[sem],
            recv_sem=self.recv_sems.at[sem],
            device_id=stream_target(stream),
            device_id_type=MESH,
        )

    def push(self, arrived):
        for pos in range(STEPS):
            for stream in range(3):
                if pos == self.started[stream] and ready_step(stream, pos) <= arrived:
                    self.copy(stream, pos).start()
                    self.started[stream] += 1

    def start(self):
        self.push(-1)

    def step(self, t):
        for stream in range(3):
            self.arrival(stream, t).wait_recv()
        self.push(t)

    def finish_sends(self):
        for stream in range(3):
            for pos in range(STEPS):
                self.copy(stream, pos).wait_send()


def needed_step(stream, back):
    owner, piece = ARRIVALS[stream][STEPS - 1 - back]
    spots = [
        STEPS - 1 - p
        for s in range(3)
        for p in range(STEPS)
        if ((SENDS[s][p][0][0], SENDS[s][p][0][1] % 4), SENDS[s][p][1]) == (owner, piece)
    ]
    return max(spots, default=-1)


class Reduce:
    def __init__(self, buf, rows, got, send_sems, recv_sems, first_sem=0):
        self.buf, self.rows, self.got = buf, rows, got
        self.send_sems, self.recv_sems, self.first = send_sems, recv_sems, first_sem
        self.started = [0, 0, 0]

    def copy(self, stream, back):
        owner, piece = ARRIVALS[stream][STEPS - 1 - back]
        sem = self.first + stream * STEPS + back
        return pltpu.make_async_remote_copy(
            src_ref=self.buf.at[tp_rank_of(owner), self.rows, cols(piece)],
            dst_ref=self.got.at[stream * STEPS + back, self.rows],
            send_sem=self.send_sems.at[sem],
            recv_sem=self.recv_sems.at[sem],
            device_id=stream_source(stream),
            device_id_type=MESH,
        )

    def push(self, arrived):
        for back in range(STEPS):
            for stream in range(3):
                if back == self.started[stream] and needed_step(stream, back) <= arrived:
                    self.copy(stream, back).start()
                    self.started[stream] += 1

    def start(self):
        self.push(-1)

    def step(self, t):
        for stream in range(3):
            self.copy(stream, t).wait_recv()
            owner, piece = SENDS[stream][STEPS - 1 - t]
            rank = tp_rank_of(owner)
            self.buf[rank, self.rows, cols(piece)] = (
                self.buf[rank, self.rows, cols(piece)].astype(jnp.float32)
                + self.got[stream * STEPS + t, self.rows].astype(jnp.float32)
            ).astype(jnp.bfloat16)
        self.push(t)

    def finish_sends(self):
        for stream in range(3):
            for back in range(STEPS):
                self.copy(stream, back).wait_send()


def gather_kernel(own_ref, out_ref, buf, send_sems, recv_sems):
    me = lax.axis_index("tp")
    buf[me] = own_ref[...]
    tp_barrier()
    gather = Gather(buf, pl.ds(0, own_ref.shape[0]), send_sems, recv_sems)
    gather.start()
    for t in range(STEPS):
        gather.step(t)
    gather.finish_sends()
    out_ref[...] = buf[...]


def gather_rows(own, collective_id):
    rows, width = own.shape
    out = pl.pallas_call(
        gather_kernel,
        out_shape=jax.ShapeDtypeStruct((8, rows, width), own.dtype),
        in_specs=[pl.BlockSpec(memory_space=pltpu.VMEM)],
        out_specs=pl.BlockSpec(memory_space=pltpu.VMEM),
        scratch_shapes=[
            pltpu.VMEM((8, rows, width), own.dtype),
            pltpu.SemaphoreType.DMA((3 * STEPS,)),
            pltpu.SemaphoreType.DMA((3 * STEPS,)),
        ],
        compiler_params=pltpu.CompilerParams(
            collective_id=collective_id, has_side_effects=True, vmem_limit_bytes=48 << 20
        ),
    )(own)
    return out.reshape(8 * rows, width)


def reduce_kernel(part_ref, out_ref, buf, got, send_sems, recv_sems):
    me = lax.axis_index("tp")
    buf[...] = part_ref[...]
    tp_barrier()
    reduction = Reduce(buf, pl.ds(0, part_ref.shape[1]), got, send_sems, recv_sems)
    reduction.start()
    for t in range(STEPS):
        reduction.step(t)
    reduction.finish_sends()
    out_ref[...] = buf[me].astype(jnp.float32)


def reduce_rows(part, collective_id):
    rows, width = part.shape[0] // 8, part.shape[1]
    return pl.pallas_call(
        reduce_kernel,
        out_shape=jax.ShapeDtypeStruct((rows, width), jnp.float32),
        in_specs=[pl.BlockSpec(memory_space=pltpu.VMEM)],
        out_specs=pl.BlockSpec(memory_space=pltpu.VMEM),
        scratch_shapes=[
            pltpu.VMEM((8, rows, width), part.dtype),
            pltpu.VMEM((3 * STEPS, rows, PIECE), part.dtype),
            pltpu.SemaphoreType.DMA((3 * STEPS,)),
            pltpu.SemaphoreType.DMA((3 * STEPS,)),
        ],
        compiler_params=pltpu.CompilerParams(
            collective_id=collective_id, has_side_effects=True, vmem_limit_bytes=48 << 20
        ),
    )(part.reshape(8, rows, width))


def shards(
    x_prompt,
    x_comp,
    up_prompt,
    up_comp,
    w_q,
    key_projection,
    value_projection,
    w_o,
    pre_gain,
    post_gain,
    dpo_weight,
    prompt_len,
    comp_len,
    loss_mask,
):
    n_tp = lax.axis_size("tp")
    pair_side = lax.axis_index("pair")
    tp_rank = lax.axis_index("tp")
    own_prompt = x_prompt[0].astype(jnp.float32)
    own_comp = x_comp[0, 0].astype(jnp.float32)
    prompt_rows = own_prompt.shape[0]
    comp_rows = own_comp.shape[0]
    row_block = prompt_rows + comp_rows
    half_rows = prompt_rows * n_tp
    comp_total = comp_rows * n_tp
    total_rows = row_block * n_tp
    prompt_total = 2 * half_rows
    length = prompt_len[0]
    own_input = jnp.concatenate([own_prompt, own_comp], axis=0)
    normed = (own_input * inverse_norm(own_input) * pre_gain).astype(jnp.bfloat16)
    gathered = gather_rows(normed, 1)
    row_ids = jnp.arange(total_rows, dtype=jnp.int32)
    row_slot = row_ids % row_block
    row_owner = row_ids // row_block
    is_prompt = row_slot < prompt_rows
    prompt_index = pair_side * half_rows + row_owner * prompt_rows + row_slot
    comp_index = row_owner * comp_rows + row_slot - prompt_rows
    positions = jnp.where(is_prompt, prompt_index, length + comp_index)
    queries = (
        rotate(jnp.dot(gathered, w_q, preferred_element_type=jnp.float32), positions, 1.0)
        * query_scale
    ).astype(jnp.bfloat16)
    key_all = rotate(
        jnp.dot(gathered, key_projection, preferred_element_type=jnp.float32), positions, 1.0
    ).astype(jnp.bfloat16)
    value_all = jnp.dot(gathered, value_projection, preferred_element_type=jnp.float32).astype(
        jnp.bfloat16
    )

    def split_rows(values):
        row_grid = values.reshape(n_tp, row_block, -1)
        return (
            row_grid[:, :prompt_rows].reshape(half_rows, -1),
            row_grid[:, prompt_rows:].reshape(comp_total, -1),
        )

    def join_rows(prompt_part, comp_part):
        prompt_grid = prompt_part.reshape(n_tp, prompt_rows, -1)
        comp_grid = comp_part.reshape(n_tp, comp_rows, -1)
        return jnp.concatenate([prompt_grid, comp_grid], axis=1).reshape(total_rows, -1)

    own_keys, comp_keys = split_rows(key_all)
    own_values, comp_values = split_rows(value_all)
    far_pack = from_partner(jnp.stack([own_keys, own_values]), "pair", 0)
    is_first_side = pair_side == 0
    prompt_keys = jnp.where(
        is_first_side,
        jnp.concatenate([own_keys, far_pack[0]], axis=0),
        jnp.concatenate([far_pack[0], own_keys], axis=0),
    )
    prompt_values = jnp.where(
        is_first_side,
        jnp.concatenate([own_values, far_pack[1]], axis=0),
        jnp.concatenate([far_pack[1], own_values], axis=0),
    )
    key_rows = jnp.concatenate([prompt_keys, comp_keys], axis=0)
    value_rows = jnp.concatenate([prompt_values, comp_values], axis=0)
    columns = jnp.arange(prompt_total + comp_total, dtype=jnp.int32)
    col_prompt = columns < prompt_total
    prompt_allowed = col_prompt[None, :] & (columns[None, :] <= prompt_index[:, None])
    comp_allowed = (col_prompt & (columns < length))[None, :] | (~col_prompt)[None, :] & (
        columns[None, :] - prompt_total <= comp_index[:, None]
    )
    allowed = jnp.where(is_prompt[:, None], prompt_allowed, comp_allowed)
    attended, probabilities, bounded, weights = attend(queries, key_rows, value_rows, allowed)
    direction = 1.0 - 2.0 * pair_side.astype(jnp.float32)
    keep_rows = jnp.concatenate(
        [jnp.ones((n_tp, prompt_rows), jnp.int32), loss_mask[0, 0].reshape(n_tp, comp_rows)], axis=1
    ).reshape(total_rows)
    row_factor = jnp.where(
        is_prompt,
        (prompt_index < length).astype(jnp.float32),
        dpo_weight[0]
        * direction
        * keep_rows.astype(jnp.float32)
        * (comp_index < comp_len[0, 0]).astype(jnp.float32),
    )
    partial_branch = jnp.dot(attended, w_o, preferred_element_type=jnp.float32)
    own_branch = reduce_rows(partial_branch.astype(jnp.bfloat16), 2)
    up_rows = jnp.concatenate([up_prompt[0], up_comp[0, 0]], axis=0)
    own_factor = lax.dynamic_slice_in_dim(row_factor, tp_rank * row_block, row_block, 0)
    grad_all = gather_rows(grad_of_branch(own_branch, up_rows, own_factor, post_gain), 3)
    output_rows = (own_input + own_branch * inverse_norm(own_branch) * post_gain).astype(
        jnp.bfloat16
    )
    out_prompt = output_rows[:prompt_rows][None]
    out_comp = output_rows[prompt_rows:][None, None]
    grad_attended = lax.dot_general(
        grad_all, w_o, (((1,), (1,)), ((), ())), preferred_element_type=jnp.float32
    ).astype(jnp.bfloat16)
    grad_queries, grad_keys, value_gradients = attend_back(
        grad_attended, queries, key_rows, value_rows, probabilities, bounded, weights
    )
    prompt_gk = grad_keys[:prompt_total]
    prompt_gv = value_gradients[:prompt_total]
    mine_k = jnp.where(is_first_side, prompt_gk[:half_rows], prompt_gk[half_rows:])
    mine_v = jnp.where(is_first_side, prompt_gv[:half_rows], prompt_gv[half_rows:])
    theirs_k = jnp.where(is_first_side, prompt_gk[half_rows:], prompt_gk[:half_rows])
    theirs_v = jnp.where(is_first_side, prompt_gv[half_rows:], prompt_gv[:half_rows])
    returned = from_partner(jnp.stack([theirs_k, theirs_v]).astype(jnp.bfloat16), "pair", 0).astype(
        jnp.float32
    )
    key_grad_rows = join_rows(mine_k + returned[0], grad_keys[prompt_total:])
    value_grad_rows = join_rows(mine_v + returned[1], value_gradients[prompt_total:])
    grad_proj = jnp.concatenate(
        [
            (rotate(grad_queries, positions, -1.0) * query_scale).astype(jnp.bfloat16),
            rotate(key_grad_rows, positions, -1.0).astype(jnp.bfloat16),
            value_grad_rows.astype(jnp.bfloat16),
        ],
        axis=1,
    )
    input_share = lax.dot_general(
        gathered, grad_proj, (((0,), (0,)), ((), ())), preferred_element_type=jnp.float32
    )
    output_term = lax.dot_general(
        grad_all, attended, (((0,), (0,)), ((), ())), preferred_element_type=jnp.float32
    )
    summed = lax.psum_scatter(
        jnp.concatenate([input_share, output_term], axis=1).astype(jnp.bfloat16),
        ("pair", "dp"),
        scatter_dimension=0,
        tiled=True,
    ).astype(jnp.float32)
    q_cols = w_q.shape[1]
    key_value_columns = key_projection.shape[1]
    grad_wq = summed[:, :q_cols]
    grad_wk = summed[:, q_cols : q_cols + key_value_columns]
    grad_wv = summed[:, q_cols + key_value_columns : q_cols + 2 * key_value_columns]
    grad_wo = summed[:, q_cols + 2 * key_value_columns :].T
    return (out_prompt, out_comp, grad_wq, grad_wk, grad_wv, grad_wo)


def solution(mesh):
    in_specs = (
        P("dp", ("pair", "tp"), None),
        P("dp", "pair", "tp", None),
        P("dp", ("pair", "tp"), None),
        P("dp", "pair", "tp", None),
        P(None, "tp"),
        P(None, "tp"),
        P(None, "tp"),
        P("tp", None),
        P(),
        P(),
        P("dp"),
        P("dp"),
        P("dp", "pair"),
        P("dp", "pair", None),
    )
    out_specs = (
        P("dp", ("pair", "tp"), None),
        P("dp", "pair", "tp", None),
        P(("pair", "dp"), "tp"),
        P(("pair", "dp"), "tp"),
        P(("pair", "dp"), "tp"),
        P("tp", ("pair", "dp")),
    )
    return jax.shard_map(shards, mesh=mesh, in_specs=in_specs, out_specs=out_specs, check_vma=False)
```

```python
import jax
import jax.numpy as jnp
from jax import lax
from jax.experimental import pallas as pl
from jax.experimental.pallas import tpu as pltpu
from jax.sharding import PartitionSpec as P

HEAD_SIZE = 128


softcap = 50.0
query_scale = 144.0 ** (-0.5)
rope_base = 10000.0
norm_eps = 1e-06


MESH = pl.DeviceIdType.MESH
PIECE = 768
PLUS, MINUS, CROSS = 0, 1, 2
STEPS = 14
SENDS = (
    [((0, 0), k) for k in (3, 4, 5, 0, 1, 2)]
    + [((0, -1), k) for k in (3, 4, 5)]
    + [((1, 0), k) for k in (3, 4)]
    + [((1, -1), k) for k in (3, 4, 5)],
    [((0, 0), k) for k in (0, 1, 2, 3, 4, 5)]
    + [((0, 1), k) for k in (0, 1, 2)]
    + [((1, 0), k) for k in (0, 1)]
    + [((1, 1), k) for k in (0, 1, 2)],
    [((0, 0), k) for k in (0, 3, 1, 4, 2, 5)]
    + [
        ((0, 1), 2),
        ((0, -1), 5),
        ((0, 1), 3),
        ((0, -1), 0),
        ((0, 1), 4),
        ((0, -1), 1),
        ((0, 1), 5),
        ((0, -1), 2),
    ],
)


def seen_from(stream, owner):
    flip, shift = owner
    if stream == CROSS:
        return (1 - flip, shift % 4)
    return (flip, (shift + (1 if stream == MINUS else -1)) % 4)


ARRIVALS = tuple(
    [(seen_from(s, owner), piece) for owner, piece in SENDS[s]] for s in range(3)
)


def ready_step(stream, pos):
    (flip, shift), piece = SENDS[stream][pos]
    if (flip, shift) == (0, 0):
        return -1
    spots = [
        p
        for s in range(3)
        for p in range(STEPS)
        if ARRIVALS[s][p] == ((flip, shift % 4), piece)
    ]
    return spots[0]


def tp_rank_of(owner):
    me = lax.axis_index("tp")
    flip, shift = owner
    return lax.rem(me // 2 + shift % 4, 4) * 2 + lax.rem(me + flip, 2)


def stream_target(stream):
    return {"tp": tp_rank_of([(0, 1), (0, 3), (1, 0)][stream])}


def stream_source(stream):
    return {"tp": tp_rank_of([(0, 3), (0, 1), (1, 0)][stream])}


def tp_barrier():
    barrier = pltpu.get_barrier_semaphore()
    for stream in range(3):
        pl.semaphore_signal(
            barrier, inc=1, device_id=stream_target(stream), device_id_type=MESH
        )
    pl.semaphore_wait(barrier, 3)


def cols(piece):
    return pl.ds(piece * PIECE, PIECE)


class Gather:
    def __init__(self, buf, rows, send_sems, recv_sems, first_sem=0):
        self.buf, self.rows = buf, rows
        self.send_sems, self.recv_sems, self.first = send_sems, recv_sems, first_sem
        self.started = [0, 0, 0]

    def copy(self, stream, pos):
        owner, piece = SENDS[stream][pos]
        ref = self.buf.at[tp_rank_of(owner), self.rows, cols(piece)]
        sem = self.first + stream * STEPS + pos
        return pltpu.make_async_remote_copy(
            src_ref=ref,
            dst_ref=ref,
            send_sem=self.send_sems.at[sem],
            recv_sem=self.recv_sems.at[sem],
            device_id=stream_target(stream),
            device_id_type=MESH,
        )

    def arrival(self, stream, pos):
        owner, piece = ARRIVALS[stream][pos]
        ref = self.buf.at[tp_rank_of(owner), self.rows, cols(piece)]
        sem = self.first + stream * STEPS + pos
        return pltpu.make_async_remote_copy(
            src_ref=ref,
            dst_ref=ref,
            send_sem=self.send_sems.at[sem],
            recv_sem=self.recv_sems.at[sem],
            device_id=stream_target(stream),
            device_id_type=MESH,
        )

    def push(self, arrived):
        for pos in range(STEPS):
            for stream in range(3):
                if pos == self.started[stream] and ready_step(stream, pos) <= arrived:
                    self.copy(stream, pos).start()
                    self.started[stream] += 1

    def start(self):
        self.push(-1)

    def step(self, t):
        for stream in range(3):
            self.arrival(stream, t).wait_recv()
        self.push(t)

    def finish_sends(self):
        for stream in range(3):
            for pos in range(STEPS):
                self.copy(stream, pos).wait_send()


def needed_step(stream, back):
    owner, piece = ARRIVALS[stream][STEPS - 1 - back]
    spots = [
        STEPS - 1 - p
        for s in range(3)
        for p in range(STEPS)
        if ((SENDS[s][p][0][0], SENDS[s][p][0][1] % 4), SENDS[s][p][1]) == (owner, piece)
    ]
    return max(spots, default=-1)


class Reduce:
    def __init__(self, buf, rows, got, send_sems, recv_sems, first_sem=0):
        self.buf, self.rows, self.got = buf, rows, got
        self.send_sems, self.recv_sems, self.first = send_sems, recv_sems, first_sem
        self.started = [0, 0, 0]

    def copy(self, stream, back):
        owner, piece = ARRIVALS[stream][STEPS - 1 - back]
        sem = self.first + stream * STEPS + back
        return pltpu.make_async_remote_copy(
            src_ref=self.buf.at[tp_rank_of(owner), self.rows, cols(piece)],
            dst_ref=self.got.at[stream * STEPS + back, self.rows],
            send_sem=self.send_sems.at[sem],
            recv_sem=self.recv_sems.at[sem],
            device_id=stream_source(stream),
            device_id_type=MESH,
        )

    def push(self, arrived):
        for back in range(STEPS):
            for stream in range(3):
                if back == self.started[stream] and needed_step(stream, back) <= arrived:
                    self.copy(stream, back).start()
                    self.started[stream] += 1

    def start(self):
        self.push(-1)

    def step(self, t):
        for stream in range(3):
            self.copy(stream, t).wait_recv()
            owner, piece = SENDS[stream][STEPS - 1 - t]
            rank = tp_rank_of(owner)
            self.buf[rank, self.rows, cols(piece)] = (
                self.buf[rank, self.rows, cols(piece)].astype(jnp.float32)
                + self.got[stream * STEPS + t, self.rows].astype(jnp.float32)
            ).astype(jnp.bfloat16)
        self.push(t)

    def finish_sends(self):
        for stream in range(3):
            for back in range(STEPS):
                self.copy(stream, back).wait_send()


class Ticker:
    def __init__(self):
        self.todo = []

    def add(self, steps):
        self.todo += steps

    def tick(self, count=1):
        for _ in range(count):
            if self.todo:
                self.todo.pop(0)()

    def drain(self):
        self.tick(len(self.todo))


def nt_dot(a, b):
    return lax.dot_general(a, b, (((1,), (1,)), ((), ())), preferred_element_type=jnp.float32)


def tn_dot(a, b):
    return lax.dot_general(a, b, (((0,), (0,)), ((), ())), preferred_element_type=jnp.float32)


def nn_dot(a, b):
    return jnp.dot(a, b, preferred_element_type=jnp.float32)


def turn(values, cosine, sine):
    return values * cosine + pltpu.roll(values, HEAD_SIZE // 2, 1) * sine


def inverse_norm(values):
    return lax.rsqrt(jnp.mean(values * values, axis=-1, keepdims=True) + norm_eps)


def iota(shape, dim):
    return lax.broadcasted_iota(jnp.int32, shape, dim)


def block_kernel(
    x_p, x_c, up_p, up_c, w_q, w_k, w_v, w_o, pre_gain, post_gain,
    cos_p, sin_p, cos_c, sin_c, dpo_weight, prompt_len, comp_len, loss_mask,
    out_p, out_c, grad_wq, grad_wk, grad_wv, grad_wo,
    xp, xc, upp, upc, wqkv, wo, nbp, nbc, brp, brc, gotp, gotc, gbp, gbc,
    qs, kv, att, prob_p, prob_c, damp_p, damp_c, dkv, dkv_out, dkv_in, gq, gkv,
    wg, core_in, up_half, up_full, down_half, down_full, pair_out, pair_in, flip,
    load_sems, tp_send, tp_recv, kv_send, kv_recv, core_send, core_recv,
    z_send, z_recv, pair_send, pair_recv,
):
    side = lax.axis_index("pair")
    me = lax.axis_index("tp")
    dp = lax.axis_index("dp")
    core, z = lax.rem(dp, 2), dp // 2
    partner = {"pair": 1 - side}
    other_core = {"dp": dp + 1 - 2 * core}
    z_up, z_down = {"dp": lax.rem(dp + 2, 16)}, {"dp": lax.rem(dp + 14, 16)}
    rows_p, rows_c = xp.shape[0], xc.shape[0]
    half, comp = 8 * rows_p, 8 * rows_c
    prompt = 2 * half
    width = xp.shape[1]
    pieces = width // PIECE

    loads = [
        pltpu.make_async_copy(source, target, load_sems.at[i])
        for i, (source, target) in enumerate(
            [
                (x_p, xp), (x_c, xc),
                (w_q, wqkv.at[:, 0:256]), (w_k, wqkv.at[:, 256:384]), (w_v, wqkv.at[:, 384:512]),
                (w_o, wo), (up_p, upp), (up_c, upc),
            ]
        )
    ]
    for load in loads:
        load.start()
    barrier = pltpu.get_barrier_semaphore()
    peers = [stream_target(s) for s in range(3)] + [partner, other_core, z_up, z_down]
    for peer in peers:
        pl.semaphore_signal(barrier, inc=1, device_id=peer, device_id_type=MESH)

    def normalize(x):
        values = x[...].astype(jnp.float32)
        return (values * inverse_norm(values) * pre_gain[...]).astype(jnp.bfloat16)

    all_p, all_c = pl.ds(0, rows_p), pl.ds(0, rows_c)
    n = 3 * STEPS
    gather_p = Gather(nbp, all_p, tp_send, tp_recv, 0)
    gather_c = Gather(nbc, all_c, tp_send, tp_recv, n)
    reduce_p = Reduce(brp, all_p, gotp, tp_send, tp_recv, 2 * n)
    reduce_c = Reduce(brc, all_c, gotc, tp_send, tp_recv, 3 * n)
    regather_p = Gather(gbp, all_p, tp_send, tp_recv, 4 * n)
    regather_c = Gather(gbc, all_c, tp_send, tp_recv, 5 * n)
    ticker = Ticker()
    tick = ticker.tick

    def steps_of(comm):
        return [lambda t=t: comm.step(t) for t in range(STEPS)]

    loads[0].wait()
    nbp[me] = normalize(xp)
    pl.semaphore_wait(barrier, len(peers))
    gather_p.start()
    loads[1].wait()
    nbc[me] = normalize(xc)
    for t in range(STEPS):
        gather_p.step(t)
        if t == 10:
            gather_c.start()
    ticker.add(steps_of(gather_c))
    for load in loads[2:5]:
        load.wait()

    def project(buf, count, every):
        total = jnp.zeros((count, 512), jnp.float32)
        for k in range(pieces):
            total += nn_dot(
                buf[:, :, k * PIECE : (k + 1) * PIECE].reshape(count, PIECE),
                wqkv[k * PIECE : (k + 1) * PIECE],
            )
            tick(every)
        return total

    def place(total, cosine, sine, first, key_first, count):
        for h in range(2):
            here = slice(h * 128, (h + 1) * 128)
            qs[first : first + count, here] = (
                turn(total[:, here], cosine[...], sine[...]) * query_scale
            ).astype(jnp.bfloat16)
        kv[key_first : key_first + count, 0:128] = turn(
            total[:, 256:384], cosine[...], sine[...]
        ).astype(jnp.bfloat16)
        kv[key_first : key_first + count, 128:256] = total[:, 384:512].astype(jnp.bfloat16)

    place(project(nbp, half, 1), cos_p, sin_p, 0, 0, half)
    kv_copy = pltpu.make_async_remote_copy(
        src_ref=kv.at[pl.ds(0, half)],
        dst_ref=kv.at[pl.ds(half, half)],
        send_sem=kv_send.at[0],
        recv_sem=kv_recv.at[0],
        device_id=partner,
        device_id_type=MESH,
    )
    kv_copy.start()
    ticker.drain()
    place(project(nbc, comp, 0), cos_c, sin_c, half, prompt, comp)
    loads[5].wait()
    kv_copy.wait_recv()

    length = prompt_len[0]

    def attend(h, first, count, keys, allowed, prob, damp):
        here = slice(h * 128, (h + 1) * 128)
        scores = nt_dot(qs[first : first + count, here], kv[0:keys, 0:128])
        bounded = jnp.tanh(scores / softcap)
        raw = jnp.where(allowed, jnp.exp(softcap * bounded), 0.0)
        probs = raw / jnp.sum(raw, axis=-1, keepdims=True)
        prob[h] = probs
        damp[h] = 1.0 - bounded * bounded
        att[first : first + count, here] = nn_dot(
            probs.astype(jnp.bfloat16), kv[0:keys, 128:256]
        ).astype(jnp.bfloat16)

    def project_out(first, count, buf, every):
        for k in range(pieces):
            here = slice(k * PIECE, (k + 1) * PIECE)
            term = nn_dot(att[first : first + count, :], wo[:, here]).astype(jnp.bfloat16)
            buf[:, :, here] = term.reshape(8, count // 8, PIECE)
            tick(every)

    row, col = iota((half, prompt), 0), iota((half, prompt), 1)
    allowed_p = ((col < half) & (col <= row)) | ((col >= half) & (side == 1))
    for h in range(2):
        attend(h, 0, half, prompt, allowed_p, prob_p, damp_p)
    project_out(0, half, brp, 0)
    reduce_p.start()
    ticker.add(steps_of(reduce_p))

    row, col = iota((comp, prompt + comp), 0), iota((comp, prompt + comp), 1)
    token = jnp.where(col < half, col + side * half, col - half + (1 - side) * half)
    allowed_c = ((col < prompt) & (token < length)) | ((col >= prompt) & (col - prompt <= row))
    for h in range(2):
        attend(h, half, comp, prompt + comp, allowed_c, prob_c, damp_c)
        tick(2)
    project_out(half, comp, brc, 1)
    tick(1)
    reduce_c.start()
    ticker.drain()

    def finish_branch(x, up, branch_rows, factor):
        branch = branch_rows.astype(jnp.float32)
        scale = inverse_norm(branch)
        out = (x[...].astype(jnp.float32) + branch * scale * post_gain[...]).astype(jnp.bfloat16)
        scaled = up[...].astype(jnp.float32) * factor * post_gain[...]
        inner = jnp.mean(branch * scaled, axis=-1, keepdims=True)
        grad = (scale * scaled - branch * (scale * scale * scale) * inner).astype(jnp.bfloat16)
        return out, grad

    loads[6].wait()
    loads[7].wait()
    token = side * half + me * rows_p + iota((rows_p, 1), 0)
    out_p[...], gbp[me] = finish_branch(xp, upp, brp[me], (token < length).astype(jnp.float32))
    regather_p.start()
    ticker.add(steps_of(reduce_c))
    ticker.drain()
    slot = iota((rows_c, 1), 0)
    keep = jnp.zeros((rows_c, 1), jnp.float32)
    for i in range(rows_c):
        keep = jnp.where(slot == i, loss_mask[me * rows_c + i].astype(jnp.float32), keep)
    direction = 1.0 - 2.0 * side.astype(jnp.float32)
    real = (me * rows_c + slot < comp_len[0]).astype(jnp.float32)
    out_c[...], gbc[me] = finish_branch(
        xc, upc, brc[me], dpo_weight[0] * direction * keep * real
    )
    for t in range(STEPS):
        regather_p.step(t)
        if t == 10:
            regather_c.start()
    ticker.add(steps_of(regather_c))

    def grad_of_attended(buf, count, every):
        total = jnp.zeros((count, 256), jnp.float32)
        for k in range(pieces):
            here = slice(k * PIECE, (k + 1) * PIECE)
            total += nt_dot(buf[:, :, here].reshape(count, PIECE), wo[:, here])
            tick(every)
        return total.astype(jnp.bfloat16)

    def attend_back(h, grad, first, count, keys, prob, damp, cosine, sine):
        here = slice(h * 128, (h + 1) * 128)
        grad_h = grad[:, here]
        grad_probs = nt_dot(grad_h, kv[0:keys, 128:256])
        probs = prob[h]
        value_part = tn_dot(probs.astype(jnp.bfloat16), grad_h)
        centered = probs * (grad_probs - jnp.sum(probs * grad_probs, axis=-1, keepdims=True))
        grad_scores = (centered * damp[h]).astype(jnp.bfloat16)
        grad_q = nn_dot(grad_scores, kv[0:keys, 0:128])
        key_part = tn_dot(grad_scores, qs[first : first + count, here])
        gq[first : first + count, here] = (
            turn(grad_q, cosine[...], -sine[...]) * query_scale
        ).astype(jnp.bfloat16)
        return key_part, value_part

    grad = grad_of_attended(gbp, half, 1)
    key_0, value_0 = attend_back(0, grad, 0, half, prompt, prob_p, damp_p, cos_p, sin_p)
    tick(3)
    key_1, value_1 = attend_back(1, grad, 0, half, prompt, prob_p, damp_p, cos_p, sin_p)
    dkv[0:prompt, 0:128] = key_0 + key_1
    dkv[0:prompt, 128:256] = value_0 + value_1
    ticker.drain()

    def weight_terms(third, left_p, left_c, right_p, right_c, every):
        per = 1152
        for j in range(width // per):
            here = slice(j * per, (j + 1) * per)
            term = tn_dot(left_p[:, :, here].reshape(half, per), right_p) + tn_dot(
                left_c[:, :, here].reshape(comp, per), right_c
            )
            wg[third, j // 2, (j % 2) * 4 : (j % 2) * 4 + 4] = (
                term.astype(jnp.bfloat16).reshape(4, 2, 144, 256)
            )
            tick(every)

    def remote(src, dst, send_sem, recv_sem, device):
        return pltpu.make_async_remote_copy(
            src_ref=src, dst_ref=dst, send_sem=send_sem, recv_sem=recv_sem,
            device_id=device, device_id_type=MESH,
        )

    sent = []

    def core_copy(third):
        return remote(
            wg.at[third, :, :, 1 - core], core_in.at[third],
            core_send.at[third], core_recv.at[third], other_core,
        )

    def start(copy):
        copy.start()
        sent.append(copy)

    def at_z(shift):
        return lax.rem(z + shift, 8)

    def z_copy(third, step, upward):
        shift = (4 - step) if upward else (4 + step)
        block = wg.at[third, :, at_z(shift), core]
        if step == 0:
            lanes = pl.ds(0 if upward else 128, 128)
            block = block.at[:, :, lanes]
            target = (up_half if upward else down_half).at[third]
        else:
            target = (up_full if upward else down_full).at[third, step - 1]
        sem = third * 8 + step * 2 + (0 if upward else 1)
        return remote(
            block, target, z_send.at[sem], z_recv.at[sem], z_up if upward else z_down
        )

    def add_core(third):
        core_copy(third).wait_recv()
        for p in range(2):
            for k in range(8):
                wg[third, p, k, core] = (
                    wg[third, p, k, core].astype(jnp.float32)
                    + core_in[third, p, k].astype(jnp.float32)
                ).astype(jnp.bfloat16)
        start(z_copy(third, 0, True))
        start(z_copy(third, 0, False))

    def z_step(third, step):
        for upward in (True, False):
            z_copy(third, step, upward).wait_recv()
            at = at_z((3 - step) if upward else (5 + step))
            if step == 0:
                lanes = slice(0, 128) if upward else slice(128, 256)
                got = (up_half if upward else down_half)[third]
                for p in range(2):
                    wg[third, p, at, core, :, lanes] = (
                        wg[third, p, at, core, :, lanes].astype(jnp.float32)
                        + got[p].astype(jnp.float32)
                    ).astype(jnp.bfloat16)
            else:
                got = (up_full if upward else down_full)[third, step - 1]
                for p in range(2):
                    wg[third, p, at, core] = (
                        wg[third, p, at, core].astype(jnp.float32) + got[p].astype(jnp.float32)
                    ).astype(jnp.bfloat16)
            start(z_copy(third, step + 1, upward))

    def pair_copy(third):
        return remote(
            pair_out.at[third], pair_in.at[third],
            pair_send.at[third], pair_recv.at[third], partner,
        )

    def z_last(third):
        z_copy(third, 3, True).wait_recv()
        z_copy(third, 3, False).wait_recv()

        def total(p):
            return (
                wg[third, p, z, core].astype(jnp.float32)
                + up_full[third, 2, p].astype(jnp.float32)
                + down_full[third, 2, p].astype(jnp.float32)
            )

        pair_out[third] = total(1 - side).astype(jnp.bfloat16)
        start(pair_copy(third))
        return total(side)

    weight_terms(0, gbp, gbc, att[0:half, :], att[half : half + comp, :], 0)
    start(core_copy(0))
    grad = grad_of_attended(gbc, comp, 0)
    add_core(0)
    parts = [
        attend_back(h, grad, half, comp, prompt + comp, prob_c, damp_c, cos_c, sin_c)
        for h in range(2)
    ]
    dkv[0:prompt, 0:128] += parts[0][0][0:prompt] + parts[1][0][0:prompt]
    dkv[0:prompt, 128:256] += parts[0][1][0:prompt] + parts[1][1][0:prompt]
    dkv_out[...] = dkv[half:prompt, :].astype(jnp.bfloat16)
    dkv_copy = remote(dkv_out, dkv_in, kv_send.at[1], kv_recv.at[1], partner)
    start(dkv_copy)
    z_step(0, 0)
    gkv[half : half + comp, 0:128] = turn(
        parts[0][0][prompt:] + parts[1][0][prompt:], cos_c[...], -sin_c[...]
    ).astype(jnp.bfloat16)
    gkv[half : half + comp, 128:256] = (parts[0][1][prompt:] + parts[1][1][prompt:]).astype(
        jnp.bfloat16
    )
    weight_terms(1, nbp, nbc, gq[0:half, :], gq[half : half + comp, :], 0)
    start(core_copy(1))
    z_step(0, 1)
    dkv_copy.wait_recv()
    whole = dkv[0:half, :] + dkv_in[...].astype(jnp.float32)
    gkv[0:half, 0:128] = turn(whole[:, 0:128], cos_p[...], -sin_p[...]).astype(jnp.bfloat16)
    gkv[0:half, 128:256] = whole[:, 128:256].astype(jnp.bfloat16)
    weight_terms(2, nbp, nbc, gkv[0:half, :], gkv[half : half + comp, :], 0)
    start(core_copy(2))
    add_core(1)
    z_step(0, 2)
    add_core(2)
    z_step(1, 0)
    z_step(2, 0)
    own_0 = z_last(0)
    z_step(1, 1)
    z_step(2, 1)
    z_step(1, 2)
    z_step(2, 2)
    pair_copy(0).wait_recv()
    flip[0:144, :] = own_0 + pair_in[0].astype(jnp.float32)
    grad_wo[...] = flip[...].T[:, 0:144]
    own_1 = z_last(1)
    own_2 = z_last(2)
    pair_copy(1).wait_recv()
    grad_wq[...] = own_1 + pair_in[1].astype(jnp.float32)
    pair_copy(2).wait_recv()
    own_2 = own_2 + pair_in[2].astype(jnp.float32)
    grad_wk[...] = own_2[:, 0:128]
    grad_wv[...] = own_2[:, 128:256]

    kv_copy.wait_send()
    for copy in sent:
        copy.wait_send()
    for comm in (gather_p, gather_c, reduce_p, reduce_c, regather_p, regather_c):
        comm.finish_sends()


def rope_tables(positions):
    half_head = HEAD_SIZE // 2
    frequencies = rope_base ** (-2.0 * jnp.arange(half_head, dtype=jnp.float32) / HEAD_SIZE)
    angles = positions.astype(jnp.float32)[:, None] * frequencies[None, :]
    cosine, sine = jnp.cos(angles), jnp.sin(angles)
    return (
        jnp.concatenate([cosine, cosine], axis=1),
        jnp.concatenate([-sine, sine], axis=1),
    )


def shards(
    x_prompt,
    x_comp,
    up_prompt,
    up_comp,
    w_q,
    key_projection,
    value_projection,
    w_o,
    pre_gain,
    post_gain,
    dpo_weight,
    prompt_len,
    comp_len,
    loss_mask,
):
    side = lax.axis_index("pair")
    rows_p, rows_c, width = x_prompt.shape[1], x_comp.shape[2], x_prompt.shape[2]
    half, comp = 8 * rows_p, 8 * rows_c
    cos_p, sin_p = rope_tables(side * half + jnp.arange(half, dtype=jnp.int32))
    cos_c, sin_c = rope_tables(prompt_len[0] + jnp.arange(comp, dtype=jnp.int32))
    bf, f32 = jnp.bfloat16, jnp.float32
    vm, anywhere, smem = (
        pl.BlockSpec(memory_space=pltpu.VMEM),
        pl.BlockSpec(memory_space=pl.ANY),
        pl.BlockSpec(memory_space=pltpu.SMEM),
    )
    dma = pltpu.SemaphoreType.DMA
    out = pl.pallas_call(
        block_kernel,
        out_shape=(
            jax.ShapeDtypeStruct((rows_p, width), bf),
            jax.ShapeDtypeStruct((rows_c, width), bf),
            jax.ShapeDtypeStruct((144, 256), f32),
            jax.ShapeDtypeStruct((144, 128), f32),
            jax.ShapeDtypeStruct((144, 128), f32),
            jax.ShapeDtypeStruct((256, 144), f32),
        ),
        in_specs=[anywhere] * 8 + [vm] * 6 + [smem] * 4,
        out_specs=[vm] * 6,
        scratch_shapes=[
            pltpu.VMEM((rows_p, width), bf),
            pltpu.VMEM((rows_c, width), bf),
            pltpu.VMEM((rows_p, width), bf),
            pltpu.VMEM((rows_c, width), bf),
            pltpu.VMEM((width, 512), bf),
            pltpu.VMEM((256, width), bf),
            pltpu.VMEM((8, rows_p, width), bf),
            pltpu.VMEM((8, rows_c, width), bf),
            pltpu.VMEM((8, rows_p, width), bf),
            pltpu.VMEM((8, rows_c, width), bf),
            pltpu.VMEM((3 * STEPS, rows_p, PIECE), bf),
            pltpu.VMEM((3 * STEPS, rows_c, PIECE), bf),
            pltpu.VMEM((8, rows_p, width), bf),
            pltpu.VMEM((8, rows_c, width), bf),
            pltpu.VMEM((half + comp, 256), bf),
            pltpu.VMEM((2 * half + comp, 256), bf),
            pltpu.VMEM((half + comp, 256), bf),
            pltpu.VMEM((2, half, 2 * half), f32),
            pltpu.VMEM((2, comp, 2 * half + comp), f32),
            pltpu.VMEM((2, half, 2 * half), f32),
            pltpu.VMEM((2, comp, 2 * half + comp), f32),
            pltpu.VMEM((2 * half, 256), f32),
            pltpu.VMEM((half, 256), bf),
            pltpu.VMEM((half, 256), bf),
            pltpu.VMEM((half + comp, 256), bf),
            pltpu.VMEM((half + comp, 256), bf),
            pltpu.VMEM((3, 2, 8, 2, 144, 256), bf),
            pltpu.VMEM((3, 2, 8, 144, 256), bf),
            pltpu.VMEM((3, 2, 144, 128), bf),
            pltpu.VMEM((3, 3, 2, 144, 256), bf),
            pltpu.VMEM((3, 2, 144, 128), bf),
            pltpu.VMEM((3, 3, 2, 144, 256), bf),
            pltpu.VMEM((3, 144, 256), bf),
            pltpu.VMEM((3, 144, 256), bf),
            pltpu.VMEM((256, 256), f32),
            dma((8,)),
            dma((18 * STEPS,)),
            dma((18 * STEPS,)),
            dma((2,)),
            dma((2,)),
            dma((3,)),
            dma((3,)),
            dma((24,)),
            dma((24,)),
            dma((3,)),
            dma((3,)),
        ],
        compiler_params=pltpu.CompilerParams(
            collective_id=1, has_side_effects=True, vmem_limit_bytes=60 << 20
        ),
        name="block",
    )(
        x_prompt[0], x_comp[0, 0], up_prompt[0], up_comp[0, 0],
        w_q, key_projection, value_projection, w_o,
        pre_gain[None], post_gain[None], cos_p, sin_p, cos_c, sin_c,
        dpo_weight, prompt_len, comp_len[0], loss_mask[0, 0],
    )
    out_p, out_c, grad_wq, grad_wk, grad_wv, grad_wo = out
    return (out_p[None], out_c[None, None], grad_wq, grad_wk, grad_wv, grad_wo)


def solution(mesh):
    in_specs = (
        P("dp", ("pair", "tp"), None),
        P("dp", "pair", "tp", None),
        P("dp", ("pair", "tp"), None),
        P("dp", "pair", "tp", None),
        P(None, "tp"),
        P(None, "tp"),
        P(None, "tp"),
        P("tp", None),
        P(),
        P(),
        P("dp"),
        P("dp"),
        P("dp", "pair"),
        P("dp", "pair", None),
    )
    out_specs = (
        P("dp", ("pair", "tp"), None),
        P("dp", "pair", "tp", None),
        P(("pair", "dp"), "tp"),
        P(("pair", "dp"), "tp"),
        P(("pair", "dp"), "tp"),
        P("tp", ("pair", "dp")),
    )
    return jax.shard_map(shards, mesh=mesh, in_specs=in_specs, out_specs=out_specs, check_vma=False)
```

```python
import jax
import numpy as np
import jax.numpy as jnp
from jax import lax
from jax.experimental import pallas as pl
from jax.experimental.pallas import tpu as pltpu
from jax.sharding import PartitionSpec as P

HEAD_SIZE = 128


softcap = 50.0
query_scale = 144.0 ** (-0.5)
rope_base = 10000.0
norm_eps = 1e-06


MESH = pl.DeviceIdType.MESH
PIECE = 768
PLUS, MINUS, CROSS = 0, 1, 2
STEPS = 14
SENDS = (
    [((0, 0), k) for k in (3, 4, 5, 0, 1, 2)]
    + [((0, -1), k) for k in (3, 4, 5)]
    + [((1, 0), k) for k in (3, 4)]
    + [((1, -1), k) for k in (3, 4, 5)],
    [((0, 0), k) for k in (0, 1, 2, 3, 4, 5)]
    + [((0, 1), k) for k in (0, 1, 2)]
    + [((1, 0), k) for k in (0, 1)]
    + [((1, 1), k) for k in (0, 1, 2)],
    [((0, 0), k) for k in (0, 3, 1, 4, 2, 5)]
    + [
        ((0, 1), 2),
        ((0, -1), 5),
        ((0, 1), 3),
        ((0, -1), 0),
        ((0, 1), 4),
        ((0, -1), 1),
        ((0, 1), 5),
        ((0, -1), 2),
    ],
)


def seen_from(stream, owner):
    flip, shift = owner
    if stream == CROSS:
        return (1 - flip, shift % 4)
    return (flip, (shift + (1 if stream == MINUS else -1)) % 4)


ARRIVALS = tuple(
    [(seen_from(s, owner), piece) for owner, piece in SENDS[s]] for s in range(3)
)


def ready_step(stream, pos):
    (flip, shift), piece = SENDS[stream][pos]
    if (flip, shift) == (0, 0):
        return -1
    spots = [
        p
        for s in range(3)
        for p in range(STEPS)
        if ARRIVALS[s][p] == ((flip, shift % 4), piece)
    ]
    return spots[0]


def tp_rank_of(owner):
    me = lax.axis_index("tp")
    flip, shift = owner
    return lax.rem(me // 2 + shift % 4, 4) * 2 + lax.rem(me + flip, 2)


def stream_target(stream):
    return {"tp": tp_rank_of([(0, 1), (0, 3), (1, 0)][stream])}


def stream_source(stream):
    return {"tp": tp_rank_of([(0, 3), (0, 1), (1, 0)][stream])}


def tp_barrier():
    barrier = pltpu.get_barrier_semaphore()
    for stream in range(3):
        pl.semaphore_signal(
            barrier, inc=1, device_id=stream_target(stream), device_id_type=MESH
        )
    pl.semaphore_wait(barrier, 3)


def cols(piece):
    return pl.ds(piece * PIECE, PIECE)


def wait_all_sends(comm):
    blocks = comm.buf.at[pl.ds(0, 7), comm.rows]
    pltpu.make_async_remote_copy(
        src_ref=blocks,
        dst_ref=blocks,
        send_sem=comm.send_sems.at[comm.first // (3 * STEPS)],
        recv_sem=comm.recv_sems.at[comm.first],
        device_id=stream_target(CROSS),
        device_id_type=MESH,
    ).wait_send()


class Gather:
    def __init__(self, buf, rows, send_sems, recv_sems, first_sem=0):
        self.buf, self.rows = buf, rows
        self.send_sems, self.recv_sems, self.first = send_sems, recv_sems, first_sem
        self.started = [0, 0, 0]

    def copy(self, stream, pos):
        owner, piece = SENDS[stream][pos]
        ref = self.buf.at[tp_rank_of(owner), self.rows, cols(piece)]
        sem = self.first + stream * STEPS + pos
        return pltpu.make_async_remote_copy(
            src_ref=ref,
            dst_ref=ref,
            send_sem=self.send_sems.at[self.first // (3 * STEPS)],
            recv_sem=self.recv_sems.at[sem],
            device_id=stream_target(stream),
            device_id_type=MESH,
        )

    def arrival(self, stream, pos):
        owner, piece = ARRIVALS[stream][pos]
        ref = self.buf.at[tp_rank_of(owner), self.rows, cols(piece)]
        sem = self.first + stream * STEPS + pos
        return pltpu.make_async_remote_copy(
            src_ref=ref,
            dst_ref=ref,
            send_sem=self.send_sems.at[self.first // (3 * STEPS)],
            recv_sem=self.recv_sems.at[sem],
            device_id=stream_target(stream),
            device_id_type=MESH,
        )

    def push(self, arrived):
        for pos in range(STEPS):
            for stream in range(3):
                if pos == self.started[stream] and ready_step(stream, pos) <= arrived:
                    self.copy(stream, pos).start()
                    self.started[stream] += 1

    def start(self):
        self.push(-1)

    def step(self, t):
        for stream in range(3):
            self.arrival(stream, t).wait_recv()
        self.push(t)

    def finish_sends(self):
        wait_all_sends(self)


def needed_step(stream, back):
    owner, piece = ARRIVALS[stream][STEPS - 1 - back]
    spots = [
        STEPS - 1 - p
        for s in range(3)
        for p in range(STEPS)
        if ((SENDS[s][p][0][0], SENDS[s][p][0][1] % 4), SENDS[s][p][1]) == (owner, piece)
    ]
    return max(spots, default=-1)


class Reduce:
    def __init__(self, buf, rows, got, send_sems, recv_sems, first_sem=0):
        self.buf, self.rows, self.got = buf, rows, got
        self.send_sems, self.recv_sems, self.first = send_sems, recv_sems, first_sem
        self.started = [0, 0, 0]

    def copy(self, stream, back):
        owner, piece = ARRIVALS[stream][STEPS - 1 - back]
        sem = self.first + stream * STEPS + back
        return pltpu.make_async_remote_copy(
            src_ref=self.buf.at[tp_rank_of(owner), self.rows, cols(piece)],
            dst_ref=self.got.at[stream * STEPS + back, self.rows],
            send_sem=self.send_sems.at[self.first // (3 * STEPS)],
            recv_sem=self.recv_sems.at[sem],
            device_id=stream_source(stream),
            device_id_type=MESH,
        )

    def push(self, arrived):
        for back in range(STEPS):
            for stream in range(3):
                if back == self.started[stream] and needed_step(stream, back) <= arrived:
                    self.copy(stream, back).start()
                    self.started[stream] += 1

    def start(self):
        self.push(-1)

    def step(self, t):
        for stream in range(3):
            self.copy(stream, t).wait_recv()
            owner, piece = SENDS[stream][STEPS - 1 - t]
            rank = tp_rank_of(owner)
            self.buf[rank, self.rows, cols(piece)] = (
                self.buf[rank, self.rows, cols(piece)].astype(jnp.float32)
                + self.got[stream * STEPS + t, self.rows].astype(jnp.float32)
            ).astype(jnp.bfloat16)
        self.push(t)

    def finish_sends(self):
        wait_all_sends(self)


class Ticker:
    def __init__(self):
        self.todo = []

    def add(self, steps):
        self.todo += steps

    def tick(self, count=1):
        for _ in range(count):
            if self.todo:
                self.todo.pop(0)()

    def drain(self):
        self.tick(len(self.todo))


def nt_dot(a, b):
    return lax.dot_general(a, b, (((1,), (1,)), ((), ())), preferred_element_type=jnp.float32)


def tn_dot(a, b):
    return lax.dot_general(a, b, (((0,), (0,)), ((), ())), preferred_element_type=jnp.float32)


def nn_dot(a, b):
    return jnp.dot(a, b, preferred_element_type=jnp.float32)


def turn(values, cosine, sine):
    return values * cosine + pltpu.roll(values, HEAD_SIZE // 2, 1) * sine


def inverse_norm(values):
    return lax.rsqrt(jnp.mean(values * values, axis=-1, keepdims=True) + norm_eps)


def iota(shape, dim):
    return lax.broadcasted_iota(jnp.int32, shape, dim)


def block_kernel(
    x_p, x_c, up_p, up_c, w_q, w_k, w_v, w_o, pre_gain, post_gain,
    rope, dpo_weight, prompt_len, comp_len, loss_mask,
    out_p, out_c, grad_wq, grad_wk, grad_wv, grad_wo,
    cos_p, sin_p, cos_c, sin_c, table, xp, xc, upp, upc, wqkv, wo, nbp, nbc, brp, brc, gotp, gotc, gbp, gbc,
    qs, kv, att, prob_p, prob_c, damp_p, damp_c, dkv, dkv_out, dkv_in, gq, gkv,
    wg, core_in, a_half, a_full, b_up, b_down, b_full, pair_out, pair_in, cross_in,
    load_sems, tp_send, tp_recv, kv_send, kv_recv, core_send, core_recv,
    z_send, z_recv, pair_send, pair_recv, cross_send, cross_recv,
):
    side = lax.axis_index("pair")
    me = lax.axis_index("tp")
    dp = lax.axis_index("dp")
    core, z = lax.rem(dp, 2), dp // 2
    partner = {"pair": 1 - side}
    other_core = {"dp": dp + 1 - 2 * core}
    z_up, z_down = {"dp": lax.rem(dp + 2, 16)}, {"dp": lax.rem(dp + 14, 16)}
    rows_p, rows_c = xp.shape[0], xc.shape[0]
    half, comp = 8 * rows_p, 8 * rows_c
    prompt = 2 * half
    width = xp.shape[1]
    pieces = width // PIECE

    loads = [
        pltpu.make_async_copy(source, target, load_sems.at[i])
        for i, (source, target) in enumerate(
            [
                (x_p, xp), (x_c, xc),
                (w_q, wqkv.at[:, 0:256]), (w_k, wqkv.at[:, 256:384]), (w_v, wqkv.at[:, 384:512]),
                (w_o, wo), (up_p, upp), (up_c, upc), (rope, table),
            ]
        )
    ]
    for load in loads:
        load.start()
    barrier = pltpu.get_barrier_semaphore()
    peers = [stream_target(s) for s in range(3)] + [partner, other_core, z_up, z_down]
    for peer in peers:
        pl.semaphore_signal(barrier, inc=1, device_id=peer, device_id_type=MESH)

    gain_in = pre_gain[...].reshape(1, width)
    gain_out = post_gain[...].reshape(1, width)

    def normalize(x):
        values = x[...].astype(jnp.float32)
        return (values * inverse_norm(values) * gain_in).astype(jnp.bfloat16)

    all_p, all_c = pl.ds(0, rows_p), pl.ds(0, rows_c)
    n = 3 * STEPS
    gather_p = Gather(nbp, all_p, tp_send, tp_recv, 0)
    gather_c = Gather(nbc, all_c, tp_send, tp_recv, n)
    reduce_p = Reduce(brp, all_p, gotp, tp_send, tp_recv, 2 * n)
    reduce_c = Reduce(brc, all_c, gotc, tp_send, tp_recv, 3 * n)
    regather_p = Gather(gbp, all_p, tp_send, tp_recv, 4 * n)
    regather_c = Gather(gbc, all_c, tp_send, tp_recv, 5 * n)
    ticker = Ticker()
    tick = ticker.tick

    def steps_of(comm):
        return [lambda t=t: comm.step(t) for t in range(STEPS)]

    loads[0].wait()
    nbp[me] = normalize(xp)
    pl.semaphore_wait(barrier, len(peers))
    gather_p.start()
    loads[1].wait()
    nbc[me] = normalize(xc)
    for t in range(STEPS):
        gather_p.step(t)
        if t == 10:
            gather_c.start()
    ticker.add(steps_of(gather_c))
    for load in loads[2:5]:
        load.wait()

    def project(buf, count, every):
        total = jnp.zeros((count, 512), jnp.float32)
        for k in range(pieces):
            total += nn_dot(
                buf[:, :, k * PIECE : (k + 1) * PIECE].reshape(count, PIECE),
                wqkv[k * PIECE : (k + 1) * PIECE],
            )
            tick(every)
        return total

    def place(total, cosine, sine, first, key_first, count):
        for h in range(2):
            here = slice(h * 128, (h + 1) * 128)
            qs[first : first + count, here] = (
                turn(total[:, here], cosine[...], sine[...]) * query_scale
            ).astype(jnp.bfloat16)
        kv[key_first : key_first + count, 0:128] = turn(
            total[:, 256:384], cosine[...], sine[...]
        ).astype(jnp.bfloat16)
        kv[key_first : key_first + count, 128:256] = total[:, 384:512].astype(jnp.bfloat16)

    loads[8].wait()
    length = prompt_len[0]

    def spread(packed, cosine, sine):
        swapped = pltpu.roll(packed, HEAD_SIZE // 2, 1)
        low = iota(packed.shape, 1) < HEAD_SIZE // 2
        cosine[...] = jnp.where(low, packed, swapped)
        sine[...] = jnp.where(low, -swapped, packed)

    spread(table[pl.ds(pl.multiple_of(side * half, half), half), :], cos_p, sin_p)
    spread(table[pl.ds(length, comp), :], cos_c, sin_c)
    place(project(nbp, half, 1), cos_p, sin_p, 0, 0, half)
    kv_copy = pltpu.make_async_remote_copy(
        src_ref=kv.at[pl.ds(0, half)],
        dst_ref=kv.at[pl.ds(half, half)],
        send_sem=kv_send.at[0],
        recv_sem=kv_recv.at[0],
        device_id=partner,
        device_id_type=MESH,
    )
    kv_copy.start()
    loads[5].wait()
    tick(4)

    def attend(h, first, count, keys, allowed, prob, damp):
        here = slice(h * 128, (h + 1) * 128)
        scores = nt_dot(qs[first : first + count, here], kv[0:keys, 0:128])
        bounded = jnp.tanh(scores / softcap)
        raw = jnp.where(allowed, jnp.exp(softcap * bounded), 0.0)
        probs = raw / jnp.sum(raw, axis=-1, keepdims=True)
        prob[h] = probs
        damp[h] = 1.0 - bounded * bounded
        att[first : first + count, here] = nn_dot(
            probs.astype(jnp.bfloat16), kv[0:keys, 128:256]
        ).astype(jnp.bfloat16)

    def project_out(first, count, buf, every):
        for k in range(pieces):
            here = slice(k * PIECE, (k + 1) * PIECE)
            term = nn_dot(att[first : first + count, :], wo[:, here]).astype(jnp.bfloat16)
            buf[:, :, here] = term.reshape(8, count // 8, PIECE)
            tick(every)

    row, col = iota((half, prompt), 0), iota((half, prompt), 1)
    allowed_p = ((col < half) & (col <= row)) | ((col >= half) & (side == 1))
    kv_copy.wait_recv()
    for h in range(2):
        attend(h, 0, half, prompt, allowed_p, prob_p, damp_p)
        tick(1)
    project_out(0, half, brp, 0)
    reduce_p.start()
    ticker.drain()
    ticker.add(steps_of(reduce_p))
    place(project(nbc, comp, 0), cos_c, sin_c, half, prompt, comp)
    tick(1)

    row, col = iota((comp, prompt + comp), 0), iota((comp, prompt + comp), 1)
    token = jnp.where(col < half, col + side * half, col - half + (1 - side) * half)
    allowed_c = ((col < prompt) & (token < length)) | ((col >= prompt) & (col - prompt <= row))
    for h in range(2):
        attend(h, half, comp, prompt + comp, allowed_c, prob_c, damp_c)
        tick(2)
    project_out(half, comp, brc, 1)
    tick(1)
    reduce_c.start()
    gather_p.finish_sends()
    gather_c.finish_sends()
    ticker.drain()

    def finish_branch(x, up, branch_rows, factor):
        branch = branch_rows.astype(jnp.float32)
        scale = inverse_norm(branch)
        out = (x[...].astype(jnp.float32) + branch * scale * gain_out).astype(jnp.bfloat16)
        scaled = up[...].astype(jnp.float32) * factor * gain_out
        inner = jnp.mean(branch * scaled, axis=-1, keepdims=True)
        grad = (scale * scaled - branch * (scale * scale * scale) * inner).astype(jnp.bfloat16)
        return out, grad

    loads[6].wait()
    loads[7].wait()
    token = side * half + me * rows_p + iota((rows_p, 1), 0)
    out_p[...], gbp[me] = finish_branch(xp, upp, brp[me], (token < length).astype(jnp.float32))
    regather_p.start()
    ticker.add(steps_of(reduce_c))
    ticker.drain()
    slot = iota((rows_c, 1), 0)
    keep = jnp.zeros((rows_c, 1), jnp.float32)
    for i in range(rows_c):
        keep = jnp.where(slot == i, loss_mask[me * rows_c + i].astype(jnp.float32), keep)
    direction = 1.0 - 2.0 * side.astype(jnp.float32)
    real = (me * rows_c + slot < comp_len[0, 0]).astype(jnp.float32)
    out_c[...], gbc[me] = finish_branch(
        xc, upc, brc[me], dpo_weight[0] * direction * keep * real
    )
    for t in range(STEPS):
        regather_p.step(t)
        if t == 10:
            regather_c.start()
            reduce_p.finish_sends()
            reduce_c.finish_sends()
    ticker.add(steps_of(regather_c))

    def grad_of_attended(buf, count, every):
        total = jnp.zeros((count, 256), jnp.float32)
        for k in range(pieces):
            here = slice(k * PIECE, (k + 1) * PIECE)
            total += nt_dot(buf[:, :, here].reshape(count, PIECE), wo[:, here])
            tick(every)
        return total.astype(jnp.bfloat16)

    def attend_back(h, grad, first, count, keys, prob, damp, cosine, sine):
        here = slice(h * 128, (h + 1) * 128)
        grad_h = grad[:, here]
        grad_probs = nt_dot(grad_h, kv[0:keys, 128:256])
        probs = prob[h]
        value_part = tn_dot(probs.astype(jnp.bfloat16), grad_h)
        centered = probs * (grad_probs - jnp.sum(probs * grad_probs, axis=-1, keepdims=True))
        grad_scores = (centered * damp[h]).astype(jnp.bfloat16)
        grad_q = nn_dot(grad_scores, kv[0:keys, 0:128])
        key_part = tn_dot(grad_scores, qs[first : first + count, here])
        gq[first : first + count, here] = (
            turn(grad_q, cosine[...], -sine[...]) * query_scale
        ).astype(jnp.bfloat16)
        return key_part, value_part

    grad = grad_of_attended(gbp, half, 1)
    key_0, value_0 = attend_back(0, grad, 0, half, prompt, prob_p, damp_p, cos_p, sin_p)
    tick(3)
    key_1, value_1 = attend_back(1, grad, 0, half, prompt, prob_p, damp_p, cos_p, sin_p)
    dkv[0:prompt, 0:128] = key_0 + key_1
    dkv[0:prompt, 128:256] = value_0 + value_1
    ticker.drain()

    def remote(src, dst, send_sem, recv_sem, device):
        return pltpu.make_async_remote_copy(
            src_ref=src, dst_ref=dst, send_sem=send_sem, recv_sem=recv_sem,
            device_id=device, device_id_type=MESH,
        )

    sent = []

    def start(copy):
        copy.start()
        sent.append(copy)

    def at_z(shift):
        return lax.rem(z + shift, 8)

    def core_copy(third, j):
        spot = (third, slice(None), j // 2, pl.ds((j % 2) * 4, 4))
        return remote(
            wg.at[spot + (1 - core,)], core_in.at[spot],
            core_send.at[third * 4 + j], core_recv.at[third * 4 + j], other_core,
        )

    def weight_terms(third, left_p, left_c, right_p, right_c):
        per = 1152
        for j in range(width // per):
            here = slice(j * per, (j + 1) * per)
            term = tn_dot(left_p[:, :, here].reshape(half, per), right_p) + tn_dot(
                left_c[:, :, here].reshape(comp, per), right_c
            )
            term = term.astype(jnp.bfloat16)
            for way in range(2):
                wg[third, way, j // 2, (j % 2) * 4 : (j % 2) * 4 + 4] = (
                    term[:, way * 128 : (way + 1) * 128].reshape(4, 2, 144, 128)
                )
            start(core_copy(third, j))

    def add_to(spot, got):
        wg[spot] = (wg[spot].astype(jnp.float32) + got.astype(jnp.float32)).astype(jnp.bfloat16)

    def add_core(third, way):
        for p in range(2):
            for k in range(8):
                add_to((third, way, p, k, core), core_in[third, way, p, k])

    def cross_copy(third):
        return remote(
            wg.at[third, 1, 1 - side, :, core], cross_in.at[third],
            cross_send.at[third], cross_recv.at[third], partner,
        )

    def add_cross(third):
        cross_copy(third).wait_recv()
        for k in range(8):
            add_to((third, 1, side, k, core), cross_in[third, k])

    def z_copy(third, way, step, upward):
        shift = (4 - step) if upward else (4 + step)
        at = at_z(shift)
        to = 0 if upward else 1
        if way == 0 and step == 0:
            block, target = wg.at[third, 0, to, at, core], a_half.at[third, to]
        elif way == 0:
            block, target = wg.at[third, 0, :, at, core], a_full.at[third, to, step - 1]
        elif step == 0:
            rows = pl.ds(0, 80) if upward else pl.ds(80, 64)
            block = wg.at[third, 1, side, at, core, rows]
            target = (b_up if upward else b_down).at[third]
        else:
            block = wg.at[third, 1, side, at, core]
            target = b_full.at[third, to, step - 1]
        sem = (third * 2 + way) * 8 + step * 2 + to
        return remote(
            block, target, z_send.at[sem], z_recv.at[sem], z_up if upward else z_down
        )

    def z_start(third, way):
        start(z_copy(third, way, 0, True))
        start(z_copy(third, way, 0, False))

    def z_step(third, way, step):
        for upward in (True, False):
            z_copy(third, way, step, upward).wait_recv()
            at = at_z((3 - step) if upward else (5 + step))
            to = 0 if upward else 1
            if way == 0 and step == 0:
                add_to((third, 0, to, at, core), a_half[third, to])
            elif way == 0:
                for p in range(2):
                    add_to(
                        (third, 0, p, at, core),
                        a_full[third, to, step - 1, p],
                    )
            elif step == 0:
                rows = pl.ds(0, 80) if upward else pl.ds(80, 64)
                add_to(
                    (third, 1, side, at, core, rows), (b_up if upward else b_down)[third]
                )
            else:
                add_to(
                    (third, 1, side, at, core), b_full[third, to, step - 1]
                )
            start(z_copy(third, way, step + 1, upward))

    def pair_copy(third):
        return remote(
            pair_out.at[third], pair_in.at[third],
            pair_send.at[third], pair_recv.at[third], partner,
        )

    def last_a(third):
        z_copy(third, 0, 3, True).wait_recv()
        z_copy(third, 0, 3, False).wait_recv()

        def total(p):
            return (
                wg[third, 0, p, z, core].astype(jnp.float32)
                + a_full[third, 0, 2, p].astype(jnp.float32)
                + a_full[third, 1, 2, p].astype(jnp.float32)
            )

        pair_out[third] = total(1 - side).astype(jnp.bfloat16)
        start(pair_copy(third))
        return total(side)

    def whole_a(third, own):
        pair_copy(third).wait_recv()
        return own + pair_in[third].astype(jnp.float32)

    def whole_b(third):
        z_copy(third, 1, 3, True).wait_recv()
        z_copy(third, 1, 3, False).wait_recv()
        return (
            wg[third, 1, side, z, core].astype(jnp.float32)
            + b_full[third, 0, 2].astype(jnp.float32)
            + b_full[third, 1, 2].astype(jnp.float32)
        )

    def turned(block):
        low = block[0:128].T
        high = jnp.concatenate([block[128:144], jnp.zeros((112, 128), jnp.float32)], axis=0).T
        return low, high[:, 0:16]

    def launch(third):
        for j in range(4):
            core_copy(third, j).wait_recv()
        add_core(third, 1)
        start(cross_copy(third))
        add_core(third, 0)
        z_start(third, 0)

    weight_terms(0, gbp, gbc, att[0:half, :], att[half : half + comp, :])
    grad = grad_of_attended(gbc, comp, 0)
    parts = [
        attend_back(h, grad, half, comp, prompt + comp, prob_c, damp_c, cos_c, sin_c)
        for h in range(2)
    ]
    dkv[0:prompt, 0:128] += parts[0][0][0:prompt] + parts[1][0][0:prompt]
    dkv[0:prompt, 128:256] += parts[0][1][0:prompt] + parts[1][1][0:prompt]
    dkv_out[...] = dkv[half:prompt, :].astype(jnp.bfloat16)
    dkv_copy = remote(dkv_out, dkv_in, kv_send.at[1], kv_recv.at[1], partner)
    start(dkv_copy)
    launch(0)
    weight_terms(1, nbp, nbc, gq[0:half, :], gq[half : half + comp, :])
    gkv[half : half + comp, 0:128] = turn(
        parts[0][0][prompt:] + parts[1][0][prompt:], cos_c[...], -sin_c[...]
    ).astype(jnp.bfloat16)
    gkv[half : half + comp, 128:256] = (parts[0][1][prompt:] + parts[1][1][prompt:]).astype(
        jnp.bfloat16
    )
    z_step(0, 0, 0)
    dkv_copy.wait_recv()
    whole = dkv[0:half, :] + dkv_in[...].astype(jnp.float32)
    gkv[0:half, 0:128] = turn(whole[:, 0:128], cos_p[...], -sin_p[...]).astype(jnp.bfloat16)
    gkv[0:half, 128:256] = whole[:, 128:256].astype(jnp.bfloat16)
    weight_terms(2, nbp, nbc, gkv[0:half, :], gkv[half : half + comp, :])
    launch(1)
    z_step(0, 0, 1)
    add_cross(0)
    z_start(0, 1)
    launch(2)
    z_step(1, 0, 0)
    z_step(0, 0, 2)
    z_step(0, 1, 0)
    z_step(2, 0, 0)
    z_step(1, 0, 1)
    add_cross(1)
    z_start(1, 1)
    own_0 = last_a(0)
    z_step(0, 1, 1)
    z_step(2, 0, 1)
    z_step(1, 0, 2)
    z_step(1, 1, 0)
    add_cross(2)
    z_start(2, 1)
    z_step(0, 1, 2)
    grad_wo[0:128, 0:128], grad_wo[0:128, 128:144] = turned(whole_a(0, own_0))
    z_step(2, 0, 2)
    own_1 = last_a(1)
    z_step(1, 1, 1)
    z_step(2, 1, 0)
    grad_wo[128:256, 0:128], grad_wo[128:256, 128:144] = turned(whole_b(0))
    own_2 = last_a(2)
    grad_wq[:, 0:128] = whole_a(1, own_1)
    z_step(1, 1, 2)
    z_step(2, 1, 1)
    grad_wk[...] = whole_a(2, own_2)
    kv_copy.wait_send()
    regather_p.finish_sends()
    regather_c.finish_sends()
    for copy in sent:
        copy.wait_send()
    sent.clear()
    grad_wq[:, 128:256] = whole_b(1)
    z_step(2, 1, 2)
    for copy in sent:
        copy.wait_send()
    grad_wv[...] = whole_b(2)


def rope_table(count):
    half_head = HEAD_SIZE // 2
    frequencies = np.power(
        np.float32(rope_base), np.float32(-2.0) * np.arange(half_head, dtype=np.float32) / HEAD_SIZE
    ).astype(np.float32)
    angles = np.arange(count, dtype=np.float32)[:, None] * frequencies[None, :]
    return np.concatenate([np.cos(angles), np.sin(angles)], axis=1).astype(np.float32)


def hand_on_kernel(*refs):
    count = len(refs) // 2
    for i in range(count):
        refs[count + i][...] = refs[i][...]


def shards(
    x_prompt,
    x_comp,
    up_prompt,
    up_comp,
    w_q,
    key_projection,
    value_projection,
    w_o,
    pre_gain,
    post_gain,
    dpo_weight,
    prompt_len,
    comp_len,
    loss_mask,
):
    rows_p, rows_c, width = x_prompt.shape[1], x_comp.shape[2], x_prompt.shape[2]
    half, comp = 8 * rows_p, 8 * rows_c
    rope = jnp.asarray(rope_table(2 * half + comp))
    bf, f32 = jnp.bfloat16, jnp.float32
    vm, anywhere, smem = (
        pl.BlockSpec(memory_space=pltpu.VMEM),
        pl.BlockSpec(memory_space=pl.ANY),
        pl.BlockSpec(memory_space=pltpu.SMEM),
    )
    dma = pltpu.SemaphoreType.DMA
    out = pl.pallas_call(
        block_kernel,
        out_shape=(
            jax.ShapeDtypeStruct((rows_p, width), bf),
            jax.ShapeDtypeStruct((rows_c, width), bf),
            jax.ShapeDtypeStruct((144, 256), f32),
            jax.ShapeDtypeStruct((144, 128), f32),
            jax.ShapeDtypeStruct((144, 128), f32),
            jax.ShapeDtypeStruct((256, 144), f32),
        ),
        in_specs=[anywhere] * 8 + [vm] * 2 + [anywhere] + [smem] * 4,
        out_specs=[vm] * 6,
        scratch_shapes=[
            pltpu.VMEM((half, 128), f32),
            pltpu.VMEM((half, 128), f32),
            pltpu.VMEM((comp, 128), f32),
            pltpu.VMEM((comp, 128), f32),
            pltpu.VMEM((2 * half + comp, 128), f32),
            pltpu.VMEM((rows_p, width), bf),
            pltpu.VMEM((rows_c, width), bf),
            pltpu.VMEM((rows_p, width), bf),
            pltpu.VMEM((rows_c, width), bf),
            pltpu.VMEM((width, 512), bf),
            pltpu.VMEM((256, width), bf),
            pltpu.VMEM((8, rows_p, width), bf),
            pltpu.VMEM((8, rows_c, width), bf),
            pltpu.VMEM((8, rows_p, width), bf),
            pltpu.VMEM((8, rows_c, width), bf),
            pltpu.VMEM((3 * STEPS, rows_p, PIECE), bf),
            pltpu.VMEM((3 * STEPS, rows_c, PIECE), bf),
            pltpu.VMEM((8, rows_p, width), bf),
            pltpu.VMEM((8, rows_c, width), bf),
            pltpu.VMEM((half + comp, 256), bf),
            pltpu.VMEM((2 * half + comp, 256), bf),
            pltpu.VMEM((half + comp, 256), bf),
            pltpu.VMEM((2, half, 2 * half), f32),
            pltpu.VMEM((2, comp, 2 * half + comp), f32),
            pltpu.VMEM((2, half, 2 * half), f32),
            pltpu.VMEM((2, comp, 2 * half + comp), f32),
            pltpu.VMEM((2 * half, 256), f32),
            pltpu.VMEM((half, 256), bf),
            pltpu.VMEM((half, 256), bf),
            pltpu.VMEM((half + comp, 256), bf),
            pltpu.VMEM((half + comp, 256), bf),
            pltpu.VMEM((3, 2, 2, 8, 2, 144, 128), bf),
            pltpu.VMEM((3, 2, 2, 8, 144, 128), bf),
            pltpu.VMEM((3, 2, 144, 128), bf),
            pltpu.VMEM((3, 2, 3, 2, 144, 128), bf),
            pltpu.VMEM((3, 80, 128), bf),
            pltpu.VMEM((3, 64, 128), bf),
            pltpu.VMEM((3, 2, 3, 144, 128), bf),
            pltpu.VMEM((3, 144, 128), bf),
            pltpu.VMEM((3, 144, 128), bf),
            pltpu.VMEM((3, 8, 144, 128), bf),
            dma((9,)),
            dma((6,)),
            dma((18 * STEPS,)),
            dma((2,)),
            dma((2,)),
            dma((12,)),
            dma((12,)),
            dma((48,)),
            dma((48,)),
            dma((3,)),
            dma((3,)),
            dma((3,)),
            dma((3,)),
        ],
        compiler_params=pltpu.CompilerParams(
            collective_id=1, has_side_effects=True, vmem_limit_bytes=60 << 20
        ),
        name="block",
    )(
        x_prompt[0], x_comp[0, 0], up_prompt[0], up_comp[0, 0],
        w_q, key_projection, value_projection, w_o,
        pre_gain, post_gain, rope,
        dpo_weight, prompt_len, comp_len, loss_mask[0, 0],
    )
    out_p, out_c, grad_wq, grad_wk, grad_wv, grad_wo = pl.pallas_call(
        hand_on_kernel,
        out_shape=tuple(jax.ShapeDtypeStruct(o.shape, o.dtype) for o in out),
        in_specs=[vm] * 6,
        out_specs=[vm] * 6,
        name="hand_on",
    )(*out)
    return (out_p[None], out_c[None, None], grad_wq, grad_wk, grad_wv, grad_wo)


def solution(mesh):
    in_specs = (
        P("dp", ("pair", "tp"), None),
        P("dp", "pair", "tp", None),
        P("dp", ("pair", "tp"), None),
        P("dp", "pair", "tp", None),
        P(None, "tp"),
        P(None, "tp"),
        P(None, "tp"),
        P("tp", None),
        P(),
        P(),
        P("dp"),
        P("dp"),
        P("dp", "pair"),
        P("dp", "pair", None),
    )
    out_specs = (
        P("dp", ("pair", "tp"), None),
        P("dp", "pair", "tp", None),
        P(("pair", "dp"), "tp"),
        P(("pair", "dp"), "tp"),
        P(("pair", "dp"), "tp"),
        P("tp", ("pair", "dp")),
    )
    return jax.shard_map(shards, mesh=mesh, in_specs=in_specs, out_specs=out_specs, check_vma=False)
```

```python
import jax
import numpy as np
import jax.numpy as jnp
from jax import lax
from jax.experimental import pallas as pl
from jax.experimental.pallas import tpu as pltpu
from jax.sharding import PartitionSpec as P

HEAD_SIZE = 128


softcap = 50.0
query_scale = 144.0 ** (-0.5)
rope_base = 10000.0
norm_eps = 1e-06


MESH = pl.DeviceIdType.MESH
PIECE = 768
PLUS, MINUS, CROSS = 0, 1, 2
STEPS = 14
SENDS = (
    [
        ((0, 0), 5),
        ((0, 0), 0),
        ((0, 0), 3),
        ((0, 0), 2),
        ((0, 0), 4),
        ((0, 0), 1),
        ((1, 0), 3),
        ((0, -1), 3),
        ((1, 0), 4),
        ((0, -1), 4),
        ((0, -1), 5),
        ((1, -1), 3),
        ((1, -1), 5),
        ((1, -1), 4),
    ],
    [
        ((0, 0), 2),
        ((0, 0), 1),
        ((0, 0), 0),
        ((0, 0), 4),
        ((0, 0), 3),
        ((0, 0), 5),
        ((1, 0), 0),
        ((0, 1), 1),
        ((1, 0), 1),
        ((0, 1), 2),
        ((0, 1), 0),
        ((1, 1), 0),
        ((1, 1), 2),
        ((1, 1), 1),
    ],
    [
        ((0, 0), 3),
        ((0, 0), 0),
        ((0, 0), 4),
        ((0, 0), 1),
        ((0, 0), 5),
        ((0, 1), 2),
        ((0, -1), 5),
        ((0, -1), 0),
        ((0, 0), 2),
        ((0, -1), 2),
        ((0, -1), 1),
        ((0, 1), 5),
        ((0, 1), 3),
        ((0, 1), 4),
    ],
)


def seen_from(stream, owner):
    flip, shift = owner
    if stream == CROSS:
        return (1 - flip, shift % 4)
    return (flip, (shift + (1 if stream == MINUS else -1)) % 4)


ARRIVALS = tuple(
    [(seen_from(s, owner), piece) for owner, piece in SENDS[s]] for s in range(3)
)


def ready_step(stream, pos):
    (flip, shift), piece = SENDS[stream][pos]
    if (flip, shift) == (0, 0):
        return -1
    spots = [
        p
        for s in range(3)
        for p in range(STEPS)
        if ARRIVALS[s][p] == ((flip, shift % 4), piece)
    ]
    return spots[0]


def tp_rank_of(owner):
    me = lax.axis_index("tp")
    flip, shift = owner
    return lax.rem(me // 2 + shift % 4, 4) * 2 + lax.rem(me + flip, 2)


def stream_target(stream):
    return {"tp": tp_rank_of([(0, 1), (0, 3), (1, 0)][stream])}


def stream_source(stream):
    return {"tp": tp_rank_of([(0, 3), (0, 1), (1, 0)][stream])}


def tp_barrier():
    barrier = pltpu.get_barrier_semaphore()
    for stream in range(3):
        pl.semaphore_signal(
            barrier, inc=1, device_id=stream_target(stream), device_id_type=MESH
        )
    pl.semaphore_wait(barrier, 3)


def cols(piece):
    return pl.ds(piece * PIECE, PIECE)


def wait_all_sends(comm):
    blocks = comm.buf.at[pl.ds(0, 7), comm.rows]
    pltpu.make_async_remote_copy(
        src_ref=blocks,
        dst_ref=blocks,
        send_sem=comm.send_sems.at[comm.first // (3 * STEPS)],
        recv_sem=comm.recv_sems.at[comm.first],
        device_id=stream_target(CROSS),
        device_id_type=MESH,
    ).wait_send()


class Gather:
    def __init__(self, buf, rows, send_sems, recv_sems, first_sem=0):
        self.buf, self.rows = buf, rows
        self.send_sems, self.recv_sems, self.first = send_sems, recv_sems, first_sem
        self.started = [0, 0, 0]

    def copy(self, stream, pos):
        owner, piece = SENDS[stream][pos]
        ref = self.buf.at[tp_rank_of(owner), self.rows, cols(piece)]
        sem = self.first + stream * STEPS + pos
        return pltpu.make_async_remote_copy(
            src_ref=ref,
            dst_ref=ref,
            send_sem=self.send_sems.at[self.first // (3 * STEPS)],
            recv_sem=self.recv_sems.at[sem],
            device_id=stream_target(stream),
            device_id_type=MESH,
        )

    def arrival(self, stream, pos):
        owner, piece = ARRIVALS[stream][pos]
        ref = self.buf.at[tp_rank_of(owner), self.rows, cols(piece)]
        sem = self.first + stream * STEPS + pos
        return pltpu.make_async_remote_copy(
            src_ref=ref,
            dst_ref=ref,
            send_sem=self.send_sems.at[self.first // (3 * STEPS)],
            recv_sem=self.recv_sems.at[sem],
            device_id=stream_target(stream),
            device_id_type=MESH,
        )

    def push(self, arrived):
        for pos in range(STEPS):
            for stream in range(3):
                if pos == self.started[stream] and ready_step(stream, pos) <= arrived:
                    self.copy(stream, pos).start()
                    self.started[stream] += 1

    def start(self):
        self.push(-1)

    def step(self, t):
        for stream in range(3):
            self.arrival(stream, t).wait_recv()
        self.push(t)

    def finish_sends(self):
        wait_all_sends(self)


def needed_step(stream, back):
    owner, piece = ARRIVALS[stream][STEPS - 1 - back]
    spots = [
        STEPS - 1 - p
        for s in range(3)
        for p in range(STEPS)
        if ((SENDS[s][p][0][0], SENDS[s][p][0][1] % 4), SENDS[s][p][1]) == (owner, piece)
    ]
    return max(spots, default=-1)


class Reduce:
    def __init__(self, buf, rows, got, send_sems, recv_sems, first_sem=0):
        self.buf, self.rows, self.got = buf, rows, got
        self.send_sems, self.recv_sems, self.first = send_sems, recv_sems, first_sem
        self.started = [0, 0, 0]

    def copy(self, stream, back):
        owner, piece = ARRIVALS[stream][STEPS - 1 - back]
        sem = self.first + stream * STEPS + back
        return pltpu.make_async_remote_copy(
            src_ref=self.buf.at[tp_rank_of(owner), self.rows, cols(piece)],
            dst_ref=self.got.at[stream * STEPS + back, self.rows],
            send_sem=self.send_sems.at[self.first // (3 * STEPS)],
            recv_sem=self.recv_sems.at[sem],
            device_id=stream_source(stream),
            device_id_type=MESH,
        )

    def push(self, arrived):
        for back in range(STEPS):
            for stream in range(3):
                if back == self.started[stream] and needed_step(stream, back) <= arrived:
                    self.copy(stream, back).start()
                    self.started[stream] += 1

    def start(self):
        self.push(-1)

    def step(self, t):
        for stream in range(3):
            self.copy(stream, t).wait_recv()
            owner, piece = SENDS[stream][STEPS - 1 - t]
            rank = tp_rank_of(owner)
            self.buf[rank, self.rows, cols(piece)] = (
                self.buf[rank, self.rows, cols(piece)].astype(jnp.float32)
                + self.got[stream * STEPS + t, self.rows].astype(jnp.float32)
            ).astype(jnp.bfloat16)
        self.push(t)

    def finish_sends(self):
        wait_all_sends(self)


class Ticker:
    def __init__(self):
        self.todo = []

    def add(self, steps):
        self.todo += steps

    def tick(self, count=1):
        for _ in range(count):
            if self.todo:
                self.todo.pop(0)()

    def drain(self):
        self.tick(len(self.todo))


def nt_dot(a, b):
    return lax.dot_general(a, b, (((1,), (1,)), ((), ())), preferred_element_type=jnp.float32)


def tn_dot(a, b):
    return lax.dot_general(a, b, (((0,), (0,)), ((), ())), preferred_element_type=jnp.float32)


def nn_dot(a, b):
    return jnp.dot(a, b, preferred_element_type=jnp.float32)


def turn(values, cosine, sine):
    return values * cosine + pltpu.roll(values, HEAD_SIZE // 2, 1) * sine


def inverse_norm(values):
    return lax.rsqrt(jnp.mean(values * values, axis=-1, keepdims=True) + norm_eps)


def iota(shape, dim):
    return lax.broadcasted_iota(jnp.int32, shape, dim)


def block_kernel(
    x_p, x_c, up_p, up_c, w_q, w_k, w_v, w_o, pre_gain, post_gain,
    rope, dpo_weight, prompt_len, comp_len, loss_mask,
    out_p, out_c, grad_wq, grad_wk, grad_wv, grad_wo,
    cos_p, sin_p, cos_c, sin_c, table, xp, xc, upp, upc, wqkv, wo, nbp, nbc, brp, brc, gotp, gotc, gbp, gbc,
    qs, kv, att, prob_p, prob_c, damp_p, damp_c, dkv, dkv_out, dkv_in, gq, gkv,
    wg, core_in, a_half, a_full, b_up, b_down, b_full, pair_out, pair_in, cross_out, cross_in,
    load_sems, tp_send, tp_recv, kv_send, kv_recv, core_send, core_recv,
    z_send, z_recv, pair_send, pair_recv, cross_send, cross_recv,
):
    side = lax.axis_index("pair")
    me = lax.axis_index("tp")
    dp = lax.axis_index("dp")
    core, z = lax.rem(dp, 2), dp // 2
    partner = {"pair": 1 - side}
    other_core = {"dp": dp + 1 - 2 * core}
    z_up, z_down = {"dp": lax.rem(dp + 2, 16)}, {"dp": lax.rem(dp + 14, 16)}
    rows_p, rows_c = xp.shape[0], xc.shape[0]
    half, comp = 8 * rows_p, 8 * rows_c
    prompt = 2 * half
    width = xp.shape[1]
    pieces = width // PIECE

    loads = [
        pltpu.make_async_copy(source, target, load_sems.at[i])
        for i, (source, target) in enumerate(
            [
                (x_p, xp), (x_c, xc),
                (w_q, wqkv.at[:, 0:256]), (w_k, wqkv.at[:, 256:384]), (w_v, wqkv.at[:, 384:512]),
                (w_o, wo), (up_p, upp), (up_c, upc), (rope, table),
            ]
        )
    ]
    for load in loads:
        load.start()
    barrier = pltpu.get_barrier_semaphore()
    peers = [stream_target(s) for s in range(3)] + [partner, other_core, z_up, z_down]
    for peer in peers:
        pl.semaphore_signal(barrier, inc=1, device_id=peer, device_id_type=MESH)

    gain_in = pre_gain[...].reshape(1, width)
    gain_out = post_gain[...].reshape(1, width)

    def normalize(x):
        values = x[...].astype(jnp.float32)
        return (values * inverse_norm(values) * gain_in).astype(jnp.bfloat16)

    all_p, all_c = pl.ds(0, rows_p), pl.ds(0, rows_c)
    n = 3 * STEPS
    gather_p = Gather(nbp, all_p, tp_send, tp_recv, 0)
    gather_c = Gather(nbc, all_c, tp_send, tp_recv, n)
    reduce_p = Reduce(brp, all_p, gotp, tp_send, tp_recv, 2 * n)
    reduce_c = Reduce(brc, all_c, gotc, tp_send, tp_recv, 3 * n)
    regather_p = Gather(gbp, all_p, tp_send, tp_recv, 4 * n)
    regather_c = Gather(gbc, all_c, tp_send, tp_recv, 5 * n)
    ticker = Ticker()
    tick = ticker.tick

    def steps_of(comm):
        return [lambda t=t: comm.step(t) for t in range(STEPS)]

    loads[0].wait()
    nbp[me] = normalize(xp)
    pl.semaphore_wait(barrier, len(peers))
    gather_p.start()
    loads[1].wait()
    nbc[me] = normalize(xc)
    for t in range(STEPS):
        gather_p.step(t)
        if t == 10:
            gather_c.start()
    ticker.add(steps_of(gather_c))
    for load in loads[2:5]:
        load.wait()

    def project(buf, count, every):
        total = jnp.zeros((count, 512), jnp.float32)
        for k in range(pieces):
            total += nn_dot(
                buf[:, :, k * PIECE : (k + 1) * PIECE].reshape(count, PIECE),
                wqkv[k * PIECE : (k + 1) * PIECE],
            )
            tick(every)
        return total

    def place(total, cosine, sine, first, key_first, count):
        for h in range(2):
            here = slice(h * 128, (h + 1) * 128)
            qs[first : first + count, here] = (
                turn(total[:, here], cosine[...], sine[...]) * query_scale
            ).astype(jnp.bfloat16)
        kv[key_first : key_first + count, 0:128] = turn(
            total[:, 256:384], cosine[...], sine[...]
        ).astype(jnp.bfloat16)
        kv[key_first : key_first + count, 128:256] = total[:, 384:512].astype(jnp.bfloat16)

    loads[8].wait()
    length = prompt_len[0]

    def spread(packed, cosine, sine):
        swapped = pltpu.roll(packed, HEAD_SIZE // 2, 1)
        low = iota(packed.shape, 1) < HEAD_SIZE // 2
        cosine[...] = jnp.where(low, packed, swapped)
        sine[...] = jnp.where(low, -swapped, packed)

    spread(table[pl.ds(pl.multiple_of(side * half, half), half), :], cos_p, sin_p)
    spread(table[pl.ds(length, comp), :], cos_c, sin_c)
    place(project(nbp, half, 1), cos_p, sin_p, 0, 0, half)
    kv_copy = pltpu.make_async_remote_copy(
        src_ref=kv.at[pl.ds(0, half)],
        dst_ref=kv.at[pl.ds(half, half)],
        send_sem=kv_send.at[0],
        recv_sem=kv_recv.at[0],
        device_id=partner,
        device_id_type=MESH,
    )
    kv_copy.start()
    loads[5].wait()
    tick(4)

    def attend(h, first, count, keys, allowed, prob, damp):
        here = slice(h * 128, (h + 1) * 128)
        scores = nt_dot(qs[first : first + count, here], kv[0:keys, 0:128])
        bounded = jnp.tanh(scores / softcap)
        raw = jnp.where(allowed, jnp.exp(softcap * bounded), 0.0)
        probs = raw / jnp.sum(raw, axis=-1, keepdims=True)
        prob[h] = probs
        damp[h] = 1.0 - bounded * bounded
        att[first : first + count, here] = nn_dot(
            probs.astype(jnp.bfloat16), kv[0:keys, 128:256]
        ).astype(jnp.bfloat16)

    def project_out(first, count, buf, every):
        for k in range(pieces):
            here = slice(k * PIECE, (k + 1) * PIECE)
            term = nn_dot(att[first : first + count, :], wo[:, here]).astype(jnp.bfloat16)
            buf[:, :, here] = term.reshape(8, count // 8, PIECE)
            tick(every)

    row, col = iota((half, prompt), 0), iota((half, prompt), 1)
    allowed_p = ((col < half) & (col <= row)) | ((col >= half) & (side == 1))
    kv_copy.wait_recv()
    for h in range(2):
        attend(h, 0, half, prompt, allowed_p, prob_p, damp_p)
        tick(1)
    project_out(0, half, brp, 0)
    reduce_p.start()
    ticker.drain()
    ticker.add(steps_of(reduce_p))
    place(project(nbc, comp, 0), cos_c, sin_c, half, prompt, comp)
    tick(1)

    row, col = iota((comp, prompt + comp), 0), iota((comp, prompt + comp), 1)
    token = jnp.where(col < half, col + side * half, col - half + (1 - side) * half)
    allowed_c = ((col < prompt) & (token < length)) | ((col >= prompt) & (col - prompt <= row))
    for h in range(2):
        attend(h, half, comp, prompt + comp, allowed_c, prob_c, damp_c)
        tick(2)
    project_out(half, comp, brc, 1)
    tick(1)
    reduce_c.start()
    gather_p.finish_sends()
    gather_c.finish_sends()
    ticker.drain()

    def finish_branch(x, up, branch_rows, factor):
        branch = branch_rows.astype(jnp.float32)
        scale = inverse_norm(branch)
        out = (x[...].astype(jnp.float32) + branch * scale * gain_out).astype(jnp.bfloat16)
        scaled = up[...].astype(jnp.float32) * factor * gain_out
        inner = jnp.mean(branch * scaled, axis=-1, keepdims=True)
        grad = (scale * scaled - branch * (scale * scale * scale) * inner).astype(jnp.bfloat16)
        return out, grad

    loads[6].wait()
    loads[7].wait()
    token = side * half + me * rows_p + iota((rows_p, 1), 0)
    out_p[...], gbp[me] = finish_branch(xp, upp, brp[me], (token < length).astype(jnp.float32))
    regather_p.start()
    ticker.add(steps_of(reduce_c))
    ticker.drain()
    slot = iota((rows_c, 1), 0)
    keep = jnp.zeros((rows_c, 1), jnp.float32)
    for i in range(rows_c):
        keep = jnp.where(slot == i, loss_mask[me * rows_c + i].astype(jnp.float32), keep)
    direction = 1.0 - 2.0 * side.astype(jnp.float32)
    real = (me * rows_c + slot < comp_len[0, 0]).astype(jnp.float32)
    out_c[...], gbc[me] = finish_branch(
        xc, upc, brc[me], dpo_weight[0] * direction * keep * real
    )
    for t in range(STEPS):
        regather_p.step(t)
        if t == 10:
            regather_c.start()
            reduce_p.finish_sends()
            reduce_c.finish_sends()
    ticker.add(steps_of(regather_c))

    def grad_of_attended(buf, count, every):
        total = jnp.zeros((count, 256), jnp.float32)
        for k in range(pieces):
            here = slice(k * PIECE, (k + 1) * PIECE)
            total += nt_dot(buf[:, :, here].reshape(count, PIECE), wo[:, here])
            tick(every)
        return total.astype(jnp.bfloat16)

    def attend_back(h, grad, first, count, keys, prob, damp, cosine, sine):
        here = slice(h * 128, (h + 1) * 128)
        grad_h = grad[:, here]
        grad_probs = nt_dot(grad_h, kv[0:keys, 128:256])
        probs = prob[h]
        value_part = tn_dot(probs.astype(jnp.bfloat16), grad_h)
        centered = probs * (grad_probs - jnp.sum(probs * grad_probs, axis=-1, keepdims=True))
        grad_scores = (centered * damp[h]).astype(jnp.bfloat16)
        grad_q = nn_dot(grad_scores, kv[0:keys, 0:128])
        key_part = tn_dot(grad_scores, qs[first : first + count, here])
        gq[first : first + count, here] = (
            turn(grad_q, cosine[...], -sine[...]) * query_scale
        ).astype(jnp.bfloat16)
        return key_part, value_part

    grad = grad_of_attended(gbp, half, 1)
    key_0, value_0 = attend_back(0, grad, 0, half, prompt, prob_p, damp_p, cos_p, sin_p)
    tick(3)
    key_1, value_1 = attend_back(1, grad, 0, half, prompt, prob_p, damp_p, cos_p, sin_p)
    dkv[0:prompt, 0:128] = key_0 + key_1
    dkv[0:prompt, 128:256] = value_0 + value_1
    ticker.drain()

    def remote(src, dst, send_sem, recv_sem, device):
        return pltpu.make_async_remote_copy(
            src_ref=src, dst_ref=dst, send_sem=send_sem, recv_sem=recv_sem,
            device_id=device, device_id_type=MESH,
        )

    sent = []

    def start(copy):
        copy.start()
        sent.append(copy)

    def at_z(shift):
        return lax.rem(z + shift, 8)

    def chunk_side(j):
        return 1 - side if j < 2 else side

    def core_copy(third, j):
        spot = (third, slice(None), chunk_side(j), pl.ds((j % 2) * 4, 4))
        return remote(
            wg.at[spot + (1 - core,)], core_in.at[spot],
            core_send.at[third * 4 + j], core_recv.at[third * 4 + j], other_core,
        )

    def weight_terms(third, left_p, left_c, right_p, right_c):
        per = 1152
        for j in range(width // per):
            here = pl.ds(pl.multiple_of((chunk_side(j) * 2 + j % 2) * per, per), per)
            term = tn_dot(left_p[:, :, here].reshape(half, per), right_p) + tn_dot(
                left_c[:, :, here].reshape(comp, per), right_c
            )
            term = term.astype(jnp.bfloat16)
            for way in range(2):
                wg[third, way, chunk_side(j), (j % 2) * 4 : (j % 2) * 4 + 4] = (
                    term[:, way * 128 : (way + 1) * 128].reshape(4, 2, 144, 128)
                )
            start(core_copy(third, j))

    def core_sum(third, way, p, at):
        return wg[third, way, p, at, core].astype(jnp.float32) + core_in[
            third, way, p, at
        ].astype(jnp.float32)

    def keep(third, way, p, at, value):
        wg[third, way, p, at, core] = value.astype(jnp.bfloat16)

    CROSS_ORDER = (4, 3, 5, 2, 6, 1, 7, 0)

    CROSS_PARTS = ((0, 3), (3, 5))

    def cross_copy(third, part):
        blocks = pl.ds(*CROSS_PARTS[part])
        return remote(
            cross_out.at[third, blocks], cross_in.at[third, blocks],
            cross_send.at[third * 2 + part], cross_recv.at[third * 2 + part], partner,
        )

    def b_sum(third, shift):
        i = CROSS_ORDER.index(shift)
        for part in range(2):
            if i == CROSS_PARTS[part][0]:
                cross_copy(third, part).wait_recv()
        return core_sum(third, 1, side, at_z(shift)) + cross_in[third, i].astype(jnp.float32)

    def z_copy(third, way, step, upward):
        shift = (4 - step) if upward else (4 + step)
        at = at_z(shift)
        to = 0 if upward else 1
        if way == 0 and step == 0:
            block, target = wg.at[third, 0, to, at, core], a_half.at[third, to]
        elif way == 0:
            block, target = wg.at[third, 0, :, at, core], a_full.at[third, to, step - 1]
        elif step == 0:
            rows = pl.ds(0, 80) if upward else pl.ds(80, 64)
            block = wg.at[third, 1, side, at, core, rows]
            target = (b_up if upward else b_down).at[third]
        else:
            block = wg.at[third, 1, side, at, core]
            target = b_full.at[third, to, step - 1]
        sem = (third * 2 + way) * 8 + step * 2 + to
        return remote(
            block, target, z_send.at[sem], z_recv.at[sem], z_up if upward else z_down
        )

    def z_start(third, way):
        if way == 0:
            for p in range(2):
                keep(third, 0, p, at_z(4), core_sum(third, 0, p, at_z(4)))
        else:
            keep(third, 1, side, at_z(4), b_sum(third, 4))
        start(z_copy(third, way, 0, True))
        start(z_copy(third, way, 0, False))

    def z_step(third, way, step):
        for upward in (True, False):
            shift = (3 - step) if upward else (5 + step)
            at = at_z(shift)
            to = 0 if upward else 1
            if way == 0:
                z_copy(third, 0, step, upward).wait_recv()
                for p in range(2):
                    value = core_sum(third, 0, p, at)
                    if step > 0:
                        value += a_full[third, to, step - 1, p].astype(jnp.float32)
                    elif p == to:
                        value += a_half[third, to].astype(jnp.float32)
                    keep(third, 0, p, at, value)
            else:
                value = b_sum(third, shift)
                z_copy(third, 1, step, upward).wait_recv()
                if step == 0 and upward:
                    arrived = jnp.concatenate(
                        [b_up[third].astype(jnp.float32), jnp.zeros((64, 128), jnp.float32)], axis=0
                    )
                elif step == 0:
                    arrived = jnp.concatenate(
                        [jnp.zeros((80, 128), jnp.float32), b_down[third].astype(jnp.float32)],
                        axis=0,
                    )
                else:
                    arrived = b_full[third, to, step - 1].astype(jnp.float32)
                keep(third, 1, side, at, value + arrived)
            start(z_copy(third, way, step + 1, upward))

    def pair_copy(third):
        return remote(
            pair_out.at[third], pair_in.at[third],
            pair_send.at[third], pair_recv.at[third], partner,
        )

    def last_a(third):
        z_copy(third, 0, 3, True).wait_recv()
        z_copy(third, 0, 3, False).wait_recv()

        def total(p):
            return (
                core_sum(third, 0, p, z)
                + a_full[third, 0, 2, p].astype(jnp.float32)
                + a_full[third, 1, 2, p].astype(jnp.float32)
            )

        pair_out[third] = total(1 - side).astype(jnp.bfloat16)
        start(pair_copy(third))
        return total(side)

    def whole_a(third, own):
        pair_copy(third).wait_recv()
        return own + pair_in[third].astype(jnp.float32)

    def whole_b(third):
        value = b_sum(third, 0)
        z_copy(third, 1, 3, True).wait_recv()
        z_copy(third, 1, 3, False).wait_recv()
        return (
            value
            + b_full[third, 0, 2].astype(jnp.float32)
            + b_full[third, 1, 2].astype(jnp.float32)
        )

    def launch_b(third):
        for j in range(2):
            core_copy(third, j).wait_recv()
        for part, (first, count) in enumerate(CROSS_PARTS):
            for i in range(first, first + count):
                cross_out[third, i] = core_sum(third, 1, 1 - side, at_z(CROSS_ORDER[i])).astype(
                    jnp.bfloat16
                )
            start(cross_copy(third, part))

    def launch_a(third):
        for j in range(2, 4):
            core_copy(third, j).wait_recv()
        z_start(third, 0)

    def settle():
        for copy in sent:
            copy.wait_send()
        sent.clear()

    weight_terms(0, gbp, gbc, att[0:half, :], att[half : half + comp, :])
    grad = grad_of_attended(gbc, comp, 0)
    parts = [
        attend_back(h, grad, half, comp, prompt + comp, prob_c, damp_c, cos_c, sin_c)
        for h in range(2)
    ]
    dkv[0:prompt, 0:128] += parts[0][0][0:prompt] + parts[1][0][0:prompt]
    dkv[0:prompt, 128:256] += parts[0][1][0:prompt] + parts[1][1][0:prompt]
    dkv_out[...] = dkv[half:prompt, :].astype(jnp.bfloat16)
    dkv_copy = remote(dkv_out, dkv_in, kv_send.at[1], kv_recv.at[1], partner)
    start(dkv_copy)
    gkv[half : half + comp, 0:128] = turn(
        parts[0][0][prompt:] + parts[1][0][prompt:], cos_c[...], -sin_c[...]
    ).astype(jnp.bfloat16)
    gkv[half : half + comp, 128:256] = (parts[0][1][prompt:] + parts[1][1][prompt:]).astype(
        jnp.bfloat16
    )
    launch_b(0)
    weight_terms(1, nbp, nbc, gq[0:half, :], gq[half : half + comp, :])
    launch_a(0)
    launch_b(1)
    launch_a(1)
    z_step(0, 0, 0)
    dkv_copy.wait_recv()
    whole = dkv[0:half, :] + dkv_in[...].astype(jnp.float32)
    gkv[0:half, 0:128] = turn(whole[:, 0:128], cos_p[...], -sin_p[...]).astype(jnp.bfloat16)
    gkv[0:half, 128:256] = whole[:, 128:256].astype(jnp.bfloat16)
    weight_terms(2, nbp, nbc, gkv[0:half, :], gkv[half : half + comp, :])
    z_start(0, 1)
    z_step(1, 0, 0)
    launch_b(2)
    z_step(0, 0, 1)
    launch_a(2)
    z_start(1, 1)
    z_step(1, 0, 1)
    z_step(0, 1, 0)
    z_step(2, 0, 0)
    z_step(1, 1, 0)
    z_step(0, 0, 2)
    z_start(2, 1)
    z_step(2, 0, 1)
    z_step(1, 1, 1)
    z_step(2, 1, 0)
    kv_copy.wait_send()
    regather_p.finish_sends()
    regather_c.finish_sends()
    z_step(1, 0, 2)
    z_step(2, 0, 2)
    z_step(0, 1, 1)
    own_0 = last_a(0)
    z_step(2, 1, 1)
    z_step(1, 1, 2)
    own_2 = last_a(2)
    z_step(0, 1, 2)
    own_1 = last_a(1)
    settle()
    z_step(2, 1, 2)
    grad_wk[...] = whole_a(2, own_2)
    grad_wo[:, 128:256] = whole_b(0)
    grad_wo[:, 0:128] = whole_a(0, own_0)
    grad_wq[:, 0:128] = whole_a(1, own_1)
    grad_wq[:, 128:256] = whole_b(1)
    settle()
    grad_wv[...] = whole_b(2)


def rope_table(count):
    half_head = HEAD_SIZE // 2
    frequencies = np.power(
        np.float32(rope_base), np.float32(-2.0) * np.arange(half_head, dtype=np.float32) / HEAD_SIZE
    ).astype(np.float32)
    angles = np.arange(count, dtype=np.float32)[:, None] * frequencies[None, :]
    return np.concatenate([np.cos(angles), np.sin(angles)], axis=1).astype(np.float32)


def hand_on_kernel(*refs):
    count = len(refs) // 2
    for i in range(count):
        refs[count + i][...] = refs[i][...]


def shards(
    x_prompt,
    x_comp,
    up_prompt,
    up_comp,
    w_q,
    key_projection,
    value_projection,
    w_o,
    pre_gain,
    post_gain,
    dpo_weight,
    prompt_len,
    comp_len,
    loss_mask,
):
    rows_p, rows_c, width = x_prompt.shape[1], x_comp.shape[2], x_prompt.shape[2]
    half, comp = 8 * rows_p, 8 * rows_c
    rope = jnp.asarray(rope_table(2 * half + comp))
    bf, f32 = jnp.bfloat16, jnp.float32
    vm, anywhere, smem = (
        pl.BlockSpec(memory_space=pltpu.VMEM),
        pl.BlockSpec(memory_space=pl.ANY),
        pl.BlockSpec(memory_space=pltpu.SMEM),
    )
    dma = pltpu.SemaphoreType.DMA
    out = pl.pallas_call(
        block_kernel,
        out_shape=(
            jax.ShapeDtypeStruct((rows_p, width), bf),
            jax.ShapeDtypeStruct((rows_c, width), bf),
            jax.ShapeDtypeStruct((144, 256), f32),
            jax.ShapeDtypeStruct((144, 128), f32),
            jax.ShapeDtypeStruct((144, 128), f32),
            jax.ShapeDtypeStruct((144, 256), f32),
        ),
        in_specs=[anywhere] * 8 + [vm] * 2 + [anywhere] + [smem] * 4,
        out_specs=[vm] * 6,
        scratch_shapes=[
            pltpu.VMEM((half, 128), f32),
            pltpu.VMEM((half, 128), f32),
            pltpu.VMEM((comp, 128), f32),
            pltpu.VMEM((comp, 128), f32),
            pltpu.VMEM((2 * half + comp, 128), f32),
            pltpu.VMEM((rows_p, width), bf),
            pltpu.VMEM((rows_c, width), bf),
            pltpu.VMEM((rows_p, width), bf),
            pltpu.VMEM((rows_c, width), bf),
            pltpu.VMEM((width, 512), bf),
            pltpu.VMEM((256, width), bf),
            pltpu.VMEM((8, rows_p, width), bf),
            pltpu.VMEM((8, rows_c, width), bf),
            pltpu.VMEM((8, rows_p, width), bf),
            pltpu.VMEM((8, rows_c, width), bf),
            pltpu.VMEM((3 * STEPS, rows_p, PIECE), bf),
            pltpu.VMEM((3 * STEPS, rows_c, PIECE), bf),
            pltpu.VMEM((8, rows_p, width), bf),
            pltpu.VMEM((8, rows_c, width), bf),
            pltpu.VMEM((half + comp, 256), bf),
            pltpu.VMEM((2 * half + comp, 256), bf),
            pltpu.VMEM((half + comp, 256), bf),
            pltpu.VMEM((2, half, 2 * half), f32),
            pltpu.VMEM((2, comp, 2 * half + comp), f32),
            pltpu.VMEM((2, half, 2 * half), f32),
            pltpu.VMEM((2, comp, 2 * half + comp), f32),
            pltpu.VMEM((2 * half, 256), f32),
            pltpu.VMEM((half, 256), bf),
            pltpu.VMEM((half, 256), bf),
            pltpu.VMEM((half + comp, 256), bf),
            pltpu.VMEM((half + comp, 256), bf),
            pltpu.VMEM((3, 2, 2, 8, 2, 144, 128), bf),
            pltpu.VMEM((3, 2, 2, 8, 144, 128), bf),
            pltpu.VMEM((3, 2, 144, 128), bf),
            pltpu.VMEM((3, 2, 3, 2, 144, 128), bf),
            pltpu.VMEM((3, 80, 128), bf),
            pltpu.VMEM((3, 64, 128), bf),
            pltpu.VMEM((3, 2, 3, 144, 128), bf),
            pltpu.VMEM((3, 144, 128), bf),
            pltpu.VMEM((3, 144, 128), bf),
            pltpu.VMEM((3, 8, 144, 128), bf),
            pltpu.VMEM((3, 8, 144, 128), bf),
            dma((9,)),
            dma((6,)),
            dma((18 * STEPS,)),
            dma((2,)),
            dma((2,)),
            dma((12,)),
            dma((12,)),
            dma((48,)),
            dma((48,)),
            dma((3,)),
            dma((3,)),
            dma((6,)),
            dma((6,)),
        ],
        compiler_params=pltpu.CompilerParams(
            collective_id=1, has_side_effects=True, vmem_limit_bytes=60 << 20
        ),
        name="block",
    )(
        x_prompt[0], x_comp[0, 0], up_prompt[0], up_comp[0, 0],
        w_q, key_projection, value_projection, w_o,
        pre_gain, post_gain, rope,
        dpo_weight, prompt_len, comp_len, loss_mask[0, 0],
    )
    out_p, out_c, grad_wq, grad_wk, grad_wv, grad_wo = pl.pallas_call(
        hand_on_kernel,
        out_shape=tuple(jax.ShapeDtypeStruct(o.shape, o.dtype) for o in out),
        in_specs=[vm] * 6,
        out_specs=[vm] * 6,
        name="hand_on",
    )(*out)
    return (out_p[None], out_c[None, None], grad_wq, grad_wk, grad_wv, grad_wo.T)


def solution(mesh):
    in_specs = (
        P("dp", ("pair", "tp"), None),
        P("dp", "pair", "tp", None),
        P("dp", ("pair", "tp"), None),
        P("dp", "pair", "tp", None),
        P(None, "tp"),
        P(None, "tp"),
        P(None, "tp"),
        P("tp", None),
        P(),
        P(),
        P("dp"),
        P("dp"),
        P("dp", "pair"),
        P("dp", "pair", None),
    )
    out_specs = (
        P("dp", ("pair", "tp"), None),
        P("dp", "pair", "tp", None),
        P(("pair", "dp"), "tp"),
        P(("pair", "dp"), "tp"),
        P(("pair", "dp"), "tp"),
        P("tp", ("pair", "dp")),
    )
    return jax.shard_map(shards, mesh=mesh, in_specs=in_specs, out_specs=out_specs, check_vma=False)
```

```python
import jax
import numpy as np
import jax.numpy as jnp
from jax import lax
from jax.experimental import pallas as pl
from jax.experimental.pallas import tpu as pltpu
from jax.sharding import PartitionSpec as P

HEAD_SIZE = 128


softcap = 50.0
query_scale = 144.0 ** (-0.5)
rope_base = 10000.0
norm_eps = 1e-06


MESH = pl.DeviceIdType.MESH
PIECE = 768
PLUS, MINUS, CROSS = 0, 1, 2
STEPS = 14
SENDS = (
    [
        ((0, 0), 5),
        ((0, 0), 0),
        ((0, 0), 3),
        ((0, 0), 2),
        ((0, 0), 4),
        ((0, 0), 1),
        ((1, 0), 3),
        ((0, -1), 3),
        ((1, 0), 4),
        ((0, -1), 4),
        ((0, -1), 5),
        ((1, -1), 3),
        ((1, -1), 5),
        ((1, -1), 4),
    ],
    [
        ((0, 0), 2),
        ((0, 0), 1),
        ((0, 0), 0),
        ((0, 0), 4),
        ((0, 0), 3),
        ((0, 0), 5),
        ((1, 0), 0),
        ((0, 1), 1),
        ((1, 0), 1),
        ((0, 1), 2),
        ((0, 1), 0),
        ((1, 1), 0),
        ((1, 1), 2),
        ((1, 1), 1),
    ],
    [
        ((0, 0), 3),
        ((0, 0), 0),
        ((0, 0), 4),
        ((0, 0), 1),
        ((0, 0), 5),
        ((0, 1), 2),
        ((0, -1), 5),
        ((0, -1), 0),
        ((0, 0), 2),
        ((0, -1), 2),
        ((0, -1), 1),
        ((0, 1), 5),
        ((0, 1), 3),
        ((0, 1), 4),
    ],
)


def seen_from(stream, owner):
    flip, shift = owner
    if stream == CROSS:
        return (1 - flip, shift % 4)
    return (flip, (shift + (1 if stream == MINUS else -1)) % 4)


ARRIVALS = tuple(
    [(seen_from(s, owner), piece) for owner, piece in SENDS[s]] for s in range(3)
)


def ready_step(stream, pos):
    (flip, shift), piece = SENDS[stream][pos]
    if (flip, shift) == (0, 0):
        return -1
    spots = [
        p
        for s in range(3)
        for p in range(STEPS)
        if ARRIVALS[s][p] == ((flip, shift % 4), piece)
    ]
    return spots[0]


def tp_rank_of(owner):
    me = lax.axis_index("tp")
    flip, shift = owner
    return lax.rem(me // 2 + shift % 4, 4) * 2 + lax.rem(me + flip, 2)


def stream_target(stream):
    return {"tp": tp_rank_of([(0, 1), (0, 3), (1, 0)][stream])}


def stream_source(stream):
    return {"tp": tp_rank_of([(0, 3), (0, 1), (1, 0)][stream])}


def tp_barrier():
    barrier = pltpu.get_barrier_semaphore()
    for stream in range(3):
        pl.semaphore_signal(
            barrier, inc=1, device_id=stream_target(stream), device_id_type=MESH
        )
    pl.semaphore_wait(barrier, 3)


def cols(piece):
    return pl.ds(piece * PIECE, PIECE)


def wait_all_sends(comm):
    blocks = comm.buf.at[pl.ds(0, 7), comm.rows]
    pltpu.make_async_remote_copy(
        src_ref=blocks,
        dst_ref=blocks,
        send_sem=comm.send_sems.at[comm.first // (3 * STEPS)],
        recv_sem=comm.recv_sems.at[comm.first],
        device_id=stream_target(CROSS),
        device_id_type=MESH,
    ).wait_send()


class Gather:
    def __init__(self, buf, rows, send_sems, recv_sems, first_sem=0):
        self.buf, self.rows = buf, rows
        self.send_sems, self.recv_sems, self.first = send_sems, recv_sems, first_sem
        self.started = [0, 0, 0]

    def copy(self, stream, pos):
        owner, piece = SENDS[stream][pos]
        ref = self.buf.at[tp_rank_of(owner), self.rows, cols(piece)]
        sem = self.first + stream * STEPS + pos
        return pltpu.make_async_remote_copy(
            src_ref=ref,
            dst_ref=ref,
            send_sem=self.send_sems.at[self.first // (3 * STEPS)],
            recv_sem=self.recv_sems.at[sem],
            device_id=stream_target(stream),
            device_id_type=MESH,
        )

    def arrival(self, stream, pos):
        owner, piece = ARRIVALS[stream][pos]
        ref = self.buf.at[tp_rank_of(owner), self.rows, cols(piece)]
        sem = self.first + stream * STEPS + pos
        return pltpu.make_async_remote_copy(
            src_ref=ref,
            dst_ref=ref,
            send_sem=self.send_sems.at[self.first // (3 * STEPS)],
            recv_sem=self.recv_sems.at[sem],
            device_id=stream_target(stream),
            device_id_type=MESH,
        )

    def push(self, arrived):
        for pos in range(STEPS):
            for stream in range(3):
                if pos == self.started[stream] and ready_step(stream, pos) <= arrived:
                    self.copy(stream, pos).start()
                    self.started[stream] += 1

    def start(self):
        self.push(-1)

    def step(self, t):
        for stream in range(3):
            self.arrival(stream, t).wait_recv()
        self.push(t)

    def finish_sends(self):
        wait_all_sends(self)


def needed_step(stream, back):
    owner, piece = ARRIVALS[stream][STEPS - 1 - back]
    spots = [
        STEPS - 1 - p
        for s in range(3)
        for p in range(STEPS)
        if ((SENDS[s][p][0][0], SENDS[s][p][0][1] % 4), SENDS[s][p][1]) == (owner, piece)
    ]
    return max(spots, default=-1)


class Reduce:
    def __init__(self, buf, rows, got, send_sems, recv_sems, first_sem=0):
        self.buf, self.rows, self.got = buf, rows, got
        self.send_sems, self.recv_sems, self.first = send_sems, recv_sems, first_sem
        self.started = [0, 0, 0]

    def copy(self, stream, back):
        owner, piece = ARRIVALS[stream][STEPS - 1 - back]
        sem = self.first + stream * STEPS + back
        return pltpu.make_async_remote_copy(
            src_ref=self.buf.at[tp_rank_of(owner), self.rows, cols(piece)],
            dst_ref=self.got.at[stream * STEPS + back, self.rows],
            send_sem=self.send_sems.at[self.first // (3 * STEPS)],
            recv_sem=self.recv_sems.at[sem],
            device_id=stream_source(stream),
            device_id_type=MESH,
        )

    def push(self, arrived):
        for back in range(STEPS):
            for stream in range(3):
                if back == self.started[stream] and needed_step(stream, back) <= arrived:
                    self.copy(stream, back).start()
                    self.started[stream] += 1

    def start(self):
        self.push(-1)

    def step(self, t):
        for stream in range(3):
            self.copy(stream, t).wait_recv()
            owner, piece = SENDS[stream][STEPS - 1 - t]
            rank = tp_rank_of(owner)
            self.buf[rank, self.rows, cols(piece)] = (
                self.buf[rank, self.rows, cols(piece)].astype(jnp.float32)
                + self.got[stream * STEPS + t, self.rows].astype(jnp.float32)
            ).astype(jnp.bfloat16)
        self.push(t)

    def finish_sends(self):
        wait_all_sends(self)


class Ticker:
    def __init__(self):
        self.todo = []

    def add(self, steps):
        self.todo += steps

    def tick(self, count=1):
        for _ in range(count):
            if self.todo:
                self.todo.pop(0)()

    def drain(self):
        self.tick(len(self.todo))


def nt_dot(a, b):
    return lax.dot_general(a, b, (((1,), (1,)), ((), ())), preferred_element_type=jnp.float32)


def tn_dot(a, b):
    return lax.dot_general(a, b, (((0,), (0,)), ((), ())), preferred_element_type=jnp.float32)


def nn_dot(a, b):
    return jnp.dot(a, b, preferred_element_type=jnp.float32)


def turn(values, cosine, sine):
    return values * cosine + pltpu.roll(values, HEAD_SIZE // 2, 1) * sine


def inverse_norm(values):
    return lax.rsqrt(jnp.mean(values * values, axis=-1, keepdims=True) + norm_eps)


def iota(shape, dim):
    return lax.broadcasted_iota(jnp.int32, shape, dim)


def block_kernel(
    x_p, x_c, up_p, up_c, w_q, w_k, w_v, w_o, pre_gain, post_gain,
    rope, dpo_weight, prompt_len, comp_len, loss_mask,
    out_p, out_c, grad_wq, grad_wk, grad_wv, grad_wo,
    cos_p, sin_p, cos_c, sin_c, table, xp, xc, upp, upc, wqkv, wo, nbp, nbc, brp, brc, gotp, gotc, gbp, gbc,
    qs, kv, att, prob_p, prob_c, damp_p, damp_c, dkv, dkv_out, dkv_in, gq, gkv,
    wg, core_in, a_half, a_full, b_up, b_down, b_full, pair_out, pair_in, cross_out, cross_in, done_p, done_c,
    load_sems, tp_send, tp_recv, kv_send, kv_recv, core_send, core_recv,
    z_send, z_recv, pair_send, pair_recv, cross_send, cross_recv, store_sems,
):
    side = lax.axis_index("pair")
    me = lax.axis_index("tp")
    dp = lax.axis_index("dp")
    core, z = lax.rem(dp, 2), dp // 2
    partner = {"pair": 1 - side}
    other_core = {"dp": dp + 1 - 2 * core}
    z_up, z_down = {"dp": lax.rem(dp + 2, 16)}, {"dp": lax.rem(dp + 14, 16)}
    rows_p, rows_c = xp.shape[0], xc.shape[0]
    half, comp = 8 * rows_p, 8 * rows_c
    prompt = 2 * half
    width = xp.shape[1]
    pieces = width // PIECE

    loads = [
        pltpu.make_async_copy(source, target, load_sems.at[i])
        for i, (source, target) in enumerate(
            [
                (x_p, xp), (x_c, xc),
                (w_q, wqkv.at[:, 0:256]), (w_k, wqkv.at[:, 256:384]), (w_v, wqkv.at[:, 384:512]),
                (w_o, wo), (up_p, upp), (up_c, upc), (rope, table),
            ]
        )
    ]
    loads[0].start()
    loads[1].start()
    barrier = pltpu.get_barrier_semaphore()
    peers = [stream_target(s) for s in range(3)] + [partner, other_core, z_up, z_down]
    for peer in peers:
        pl.semaphore_signal(barrier, inc=1, device_id=peer, device_id_type=MESH)

    gain_in = pre_gain[...].reshape(1, width)
    gain_out = post_gain[...].reshape(1, width)

    def normalize(x):
        values = x[...].astype(jnp.float32)
        return (values * inverse_norm(values) * gain_in).astype(jnp.bfloat16)

    all_p, all_c = pl.ds(0, rows_p), pl.ds(0, rows_c)
    n = 3 * STEPS
    gather_p = Gather(nbp, all_p, tp_send, tp_recv, 0)
    gather_c = Gather(nbc, all_c, tp_send, tp_recv, n)
    reduce_p = Reduce(brp, all_p, gotp, tp_send, tp_recv, 2 * n)
    reduce_c = Reduce(brc, all_c, gotc, tp_send, tp_recv, 3 * n)
    regather_p = Gather(gbp, all_p, tp_send, tp_recv, 4 * n)
    regather_c = Gather(gbc, all_c, tp_send, tp_recv, 5 * n)
    ticker = Ticker()
    tick = ticker.tick

    def steps_of(comm):
        return [lambda t=t: comm.step(t) for t in range(STEPS)]

    loads[0].wait()
    nbp[me] = normalize(xp)
    pl.semaphore_wait(barrier, len(peers))
    gather_p.start()
    for load in loads[2:]:
        load.start()
    loads[1].wait()
    nbc[me] = normalize(xc)
    for t in range(STEPS):
        gather_p.step(t)
        if t == 10:
            gather_c.start()
    ticker.add(steps_of(gather_c))
    for load in loads[2:5]:
        load.wait()

    def project(buf, count, every):
        total = jnp.zeros((count, 512), jnp.float32)
        for k in range(pieces):
            total += nn_dot(
                buf[:, :, k * PIECE : (k + 1) * PIECE].reshape(count, PIECE),
                wqkv[k * PIECE : (k + 1) * PIECE],
            )
            tick(every)
        return total

    def place(total, cosine, sine, first, key_first, count):
        for h in range(2):
            here = slice(h * 128, (h + 1) * 128)
            qs[first : first + count, here] = (
                turn(total[:, here], cosine[...], sine[...]) * query_scale
            ).astype(jnp.bfloat16)
        kv[key_first : key_first + count, 0:128] = turn(
            total[:, 256:384], cosine[...], sine[...]
        ).astype(jnp.bfloat16)
        kv[key_first : key_first + count, 128:256] = total[:, 384:512].astype(jnp.bfloat16)

    loads[8].wait()
    length = prompt_len[0]

    def spread(packed, cosine, sine):
        swapped = pltpu.roll(packed, HEAD_SIZE // 2, 1)
        low = iota(packed.shape, 1) < HEAD_SIZE // 2
        cosine[...] = jnp.where(low, packed, swapped)
        sine[...] = jnp.where(low, -swapped, packed)

    spread(table[pl.ds(pl.multiple_of(side * half, half), half), :], cos_p, sin_p)
    spread(table[pl.ds(length, comp), :], cos_c, sin_c)
    place(project(nbp, half, 1), cos_p, sin_p, 0, 0, half)
    kv_copy = pltpu.make_async_remote_copy(
        src_ref=kv.at[pl.ds(0, half)],
        dst_ref=kv.at[pl.ds(half, half)],
        send_sem=kv_send.at[0],
        recv_sem=kv_recv.at[0],
        device_id=partner,
        device_id_type=MESH,
    )
    kv_copy.start()
    loads[5].wait()
    tick(4)

    def attend(h, first, count, keys, allowed, prob, damp):
        here = slice(h * 128, (h + 1) * 128)
        scores = nt_dot(qs[first : first + count, here], kv[0:keys, 0:128])
        bounded = jnp.tanh(scores / softcap)
        raw = jnp.where(allowed, jnp.exp(softcap * bounded), 0.0)
        probs = raw / jnp.sum(raw, axis=-1, keepdims=True)
        prob[h] = probs
        damp[h] = 1.0 - bounded * bounded
        att[first : first + count, here] = nn_dot(
            probs.astype(jnp.bfloat16), kv[0:keys, 128:256]
        ).astype(jnp.bfloat16)

    def project_out(first, count, buf, every):
        for k in range(pieces):
            here = slice(k * PIECE, (k + 1) * PIECE)
            term = nn_dot(att[first : first + count, :], wo[:, here]).astype(jnp.bfloat16)
            buf[:, :, here] = term.reshape(8, count // 8, PIECE)
            tick(every)

    row, col = iota((half, prompt), 0), iota((half, prompt), 1)
    allowed_p = ((col < half) & (col <= row)) | ((col >= half) & (side == 1))
    kv_copy.wait_recv()
    for h in range(2):
        attend(h, 0, half, prompt, allowed_p, prob_p, damp_p)
        tick(1)
    project_out(0, half, brp, 0)
    reduce_p.start()
    ticker.drain()
    ticker.add(steps_of(reduce_p))
    place(project(nbc, comp, 0), cos_c, sin_c, half, prompt, comp)
    tick(1)

    row, col = iota((comp, prompt + comp), 0), iota((comp, prompt + comp), 1)
    token = jnp.where(col < half, col + side * half, col - half + (1 - side) * half)
    allowed_c = ((col < prompt) & (token < length)) | ((col >= prompt) & (col - prompt <= row))
    for h in range(2):
        attend(h, half, comp, prompt + comp, allowed_c, prob_c, damp_c)
        tick(2)
    project_out(half, comp, brc, 1)
    tick(1)
    reduce_c.start()
    gather_p.finish_sends()
    gather_c.finish_sends()
    ticker.drain()

    def finish_branch(x, up, branch_rows, factor):
        branch = branch_rows.astype(jnp.float32)
        scale = inverse_norm(branch)
        out = (x[...].astype(jnp.float32) + branch * scale * gain_out).astype(jnp.bfloat16)
        scaled = up[...].astype(jnp.float32) * factor * gain_out
        inner = jnp.mean(branch * scaled, axis=-1, keepdims=True)
        grad = (scale * scaled - branch * (scale * scale * scale) * inner).astype(jnp.bfloat16)
        return out, grad

    loads[6].wait()
    loads[7].wait()
    token = side * half + me * rows_p + iota((rows_p, 1), 0)
    done_p[...], gbp[me] = finish_branch(xp, upp, brp[me], (token < length).astype(jnp.float32))
    regather_p.start()
    store_p = pltpu.make_async_copy(done_p, out_p, store_sems.at[0])
    store_p.start()
    for t in range(STEPS):
        reduce_c.step(t)
        if t >= 8:
            regather_p.step(t - 8)
    slot = iota((rows_c, 1), 0)
    keep = jnp.zeros((rows_c, 1), jnp.float32)
    for i in range(rows_c):
        keep = jnp.where(slot == i, loss_mask[me * rows_c + i].astype(jnp.float32), keep)
    direction = 1.0 - 2.0 * side.astype(jnp.float32)
    real = (me * rows_c + slot < comp_len[0, 0]).astype(jnp.float32)
    done_c[...], gbc[me] = finish_branch(
        xc, upc, brc[me], dpo_weight[0] * direction * keep * real
    )
    store_c = pltpu.make_async_copy(done_c, out_c, store_sems.at[1])
    store_c.start()
    for t in range(STEPS - 8, STEPS):
        regather_p.step(t)
        if t == 10:
            regather_c.start()
            reduce_p.finish_sends()
            reduce_c.finish_sends()
    ticker.add(steps_of(regather_c))

    def grad_of_attended(buf, count, every):
        total = jnp.zeros((count, 256), jnp.float32)
        for k in range(pieces):
            here = slice(k * PIECE, (k + 1) * PIECE)
            total += nt_dot(buf[:, :, here].reshape(count, PIECE), wo[:, here])
            tick(every)
        return total.astype(jnp.bfloat16)

    def attend_back(h, grad, first, count, keys, prob, damp, cosine, sine):
        here = slice(h * 128, (h + 1) * 128)
        grad_h = grad[:, here]
        grad_probs = nt_dot(grad_h, kv[0:keys, 128:256])
        probs = prob[h]
        value_part = tn_dot(probs.astype(jnp.bfloat16), grad_h)
        centered = probs * (grad_probs - jnp.sum(probs * grad_probs, axis=-1, keepdims=True))
        grad_scores = (centered * damp[h]).astype(jnp.bfloat16)
        grad_q = nn_dot(grad_scores, kv[0:keys, 0:128])
        key_part = tn_dot(grad_scores, qs[first : first + count, here])
        gq[first : first + count, here] = (
            turn(grad_q, cosine[...], -sine[...]) * query_scale
        ).astype(jnp.bfloat16)
        return key_part, value_part

    grad = grad_of_attended(gbp, half, 1)
    key_0, value_0 = attend_back(0, grad, 0, half, prompt, prob_p, damp_p, cos_p, sin_p)
    tick(3)
    key_1, value_1 = attend_back(1, grad, 0, half, prompt, prob_p, damp_p, cos_p, sin_p)
    dkv[0:prompt, 0:128] = key_0 + key_1
    dkv[0:prompt, 128:256] = value_0 + value_1
    ticker.drain()

    def remote(src, dst, send_sem, recv_sem, device):
        return pltpu.make_async_remote_copy(
            src_ref=src, dst_ref=dst, send_sem=send_sem, recv_sem=recv_sem,
            device_id=device, device_id_type=MESH,
        )

    sent = []

    def start(copy):
        copy.start()
        sent.append(copy)

    def at_z(shift):
        return lax.rem(z + shift, 8)

    def chunk_side(j):
        return 1 - side if j < 2 else side

    def core_copy(third, j):
        spot = (third, slice(None), chunk_side(j), pl.ds((j % 2) * 4, 4))
        return remote(
            wg.at[spot + (1 - core,)], core_in.at[spot],
            core_send.at[third * 4 + j], core_recv.at[third * 4 + j], other_core,
        )

    def weight_terms(third, left_p, left_c, right_p, right_c):
        per = 1152
        for j in range(width // per):
            here = pl.ds(pl.multiple_of((chunk_side(j) * 2 + j % 2) * per, per), per)
            term = tn_dot(left_p[:, :, here].reshape(half, per), right_p) + tn_dot(
                left_c[:, :, here].reshape(comp, per), right_c
            )
            term = term.astype(jnp.bfloat16)
            for way in range(2):
                wg[third, way, chunk_side(j), (j % 2) * 4 : (j % 2) * 4 + 4] = (
                    term[:, way * 128 : (way + 1) * 128].reshape(4, 2, 144, 128)
                )
            start(core_copy(third, j))

    def core_sum(third, way, p, at):
        return wg[third, way, p, at, core].astype(jnp.float32) + core_in[
            third, way, p, at
        ].astype(jnp.float32)

    def keep(third, way, p, at, value):
        wg[third, way, p, at, core] = value.astype(jnp.bfloat16)

    CROSS_ORDER = (4, 3, 5, 2, 6, 1, 7, 0)

    CROSS_PARTS = ((0, 3), (3, 5))

    def cross_copy(third, part):
        blocks = pl.ds(*CROSS_PARTS[part])
        return remote(
            cross_out.at[third, blocks], cross_in.at[third, blocks],
            cross_send.at[third * 2 + part], cross_recv.at[third * 2 + part], partner,
        )

    def b_sum(third, shift):
        i = CROSS_ORDER.index(shift)
        for part in range(2):
            if i == CROSS_PARTS[part][0]:
                cross_copy(third, part).wait_recv()
        return core_sum(third, 1, side, at_z(shift)) + cross_in[third, i].astype(jnp.float32)

    def z_copy(third, way, step, upward):
        shift = (4 - step) if upward else (4 + step)
        at = at_z(shift)
        to = 0 if upward else 1
        if way == 0 and step == 0:
            block, target = wg.at[third, 0, to, at, core], a_half.at[third, to]
        elif way == 0:
            block, target = wg.at[third, 0, :, at, core], a_full.at[third, to, step - 1]
        elif step == 0:
            rows = pl.ds(0, 80) if upward else pl.ds(80, 64)
            block = wg.at[third, 1, side, at, core, rows]
            target = (b_up if upward else b_down).at[third]
        else:
            block = wg.at[third, 1, side, at, core]
            target = b_full.at[third, to, step - 1]
        sem = (third * 2 + way) * 8 + step * 2 + to
        return remote(
            block, target, z_send.at[sem], z_recv.at[sem], z_up if upward else z_down
        )

    def z_start(third, way):
        if way == 0:
            for p in range(2):
                keep(third, 0, p, at_z(4), core_sum(third, 0, p, at_z(4)))
        else:
            keep(third, 1, side, at_z(4), b_sum(third, 4))
        start(z_copy(third, way, 0, True))
        start(z_copy(third, way, 0, False))

    def z_step(third, way, step):
        for upward in (True, False):
            shift = (3 - step) if upward else (5 + step)
            at = at_z(shift)
            to = 0 if upward else 1
            if way == 0:
                z_copy(third, 0, step, upward).wait_recv()
                for p in range(2):
                    value = core_sum(third, 0, p, at)
                    if step > 0:
                        value += a_full[third, to, step - 1, p].astype(jnp.float32)
                    elif p == to:
                        value += a_half[third, to].astype(jnp.float32)
                    keep(third, 0, p, at, value)
            else:
                value = b_sum(third, shift)
                z_copy(third, 1, step, upward).wait_recv()
                if step == 0 and upward:
                    arrived = jnp.concatenate(
                        [b_up[third].astype(jnp.float32), jnp.zeros((64, 128), jnp.float32)], axis=0
                    )
                elif step == 0:
                    arrived = jnp.concatenate(
                        [jnp.zeros((80, 128), jnp.float32), b_down[third].astype(jnp.float32)],
                        axis=0,
                    )
                else:
                    arrived = b_full[third, to, step - 1].astype(jnp.float32)
                keep(third, 1, side, at, value + arrived)
            start(z_copy(third, way, step + 1, upward))

    def pair_copy(third):
        return remote(
            pair_out.at[third], pair_in.at[third],
            pair_send.at[third], pair_recv.at[third], partner,
        )

    def last_a(third):
        z_copy(third, 0, 3, True).wait_recv()
        z_copy(third, 0, 3, False).wait_recv()

        def total(p):
            return (
                core_sum(third, 0, p, z)
                + a_full[third, 0, 2, p].astype(jnp.float32)
                + a_full[third, 1, 2, p].astype(jnp.float32)
            )

        pair_out[third] = total(1 - side).astype(jnp.bfloat16)
        start(pair_copy(third))
        return total(side)

    def whole_a(third, own):
        pair_copy(third).wait_recv()
        return own + pair_in[third].astype(jnp.float32)

    def whole_b(third):
        value = b_sum(third, 0)
        z_copy(third, 1, 3, True).wait_recv()
        z_copy(third, 1, 3, False).wait_recv()
        return (
            value
            + b_full[third, 0, 2].astype(jnp.float32)
            + b_full[third, 1, 2].astype(jnp.float32)
        )

    def launch_b(third):
        for j in range(2):
            core_copy(third, j).wait_recv()
        for part, (first, count) in enumerate(CROSS_PARTS):
            for i in range(first, first + count):
                cross_out[third, i] = core_sum(third, 1, 1 - side, at_z(CROSS_ORDER[i])).astype(
                    jnp.bfloat16
                )
            start(cross_copy(third, part))

    def launch_a(third):
        for j in range(2, 4):
            core_copy(third, j).wait_recv()
        z_start(third, 0)

    def settle():
        for copy in sent:
            copy.wait_send()
        sent.clear()

    weight_terms(0, gbp, gbc, att[0:half, :], att[half : half + comp, :])
    grad = grad_of_attended(gbc, comp, 0)
    parts = [
        attend_back(h, grad, half, comp, prompt + comp, prob_c, damp_c, cos_c, sin_c)
        for h in range(2)
    ]
    dkv[0:prompt, 0:128] += parts[0][0][0:prompt] + parts[1][0][0:prompt]
    dkv[0:prompt, 128:256] += parts[0][1][0:prompt] + parts[1][1][0:prompt]
    dkv_out[...] = dkv[half:prompt, :].astype(jnp.bfloat16)
    dkv_copy = remote(dkv_out, dkv_in, kv_send.at[1], kv_recv.at[1], partner)
    start(dkv_copy)
    gkv[half : half + comp, 0:128] = turn(
        parts[0][0][prompt:] + parts[1][0][prompt:], cos_c[...], -sin_c[...]
    ).astype(jnp.bfloat16)
    gkv[half : half + comp, 128:256] = (parts[0][1][prompt:] + parts[1][1][prompt:]).astype(
        jnp.bfloat16
    )
    launch_b(0)
    weight_terms(1, nbp, nbc, gq[0:half, :], gq[half : half + comp, :])
    launch_a(0)
    launch_b(1)
    launch_a(1)
    z_step(0, 0, 0)
    dkv_copy.wait_recv()
    whole = dkv[0:half, :] + dkv_in[...].astype(jnp.float32)
    gkv[0:half, 0:128] = turn(whole[:, 0:128], cos_p[...], -sin_p[...]).astype(jnp.bfloat16)
    gkv[0:half, 128:256] = whole[:, 128:256].astype(jnp.bfloat16)
    weight_terms(2, nbp, nbc, gkv[0:half, :], gkv[half : half + comp, :])
    z_start(0, 1)
    z_step(1, 0, 0)
    launch_b(2)
    z_step(0, 0, 1)
    launch_a(2)
    z_start(1, 1)
    z_step(1, 0, 1)
    z_step(0, 1, 0)
    z_step(2, 0, 0)
    z_step(1, 1, 0)
    z_step(0, 0, 2)
    z_start(2, 1)
    z_step(2, 0, 1)
    z_step(1, 1, 1)
    z_step(2, 1, 0)
    store_p.wait()
    store_c.wait()
    kv_copy.wait_send()
    regather_p.finish_sends()
    regather_c.finish_sends()
    z_step(1, 0, 2)
    z_step(2, 0, 2)
    z_step(0, 1, 1)
    own_0 = last_a(0)
    z_step(2, 1, 1)
    z_step(1, 1, 2)
    own_2 = last_a(2)
    z_step(0, 1, 2)
    own_1 = last_a(1)
    settle()
    z_step(2, 1, 2)
    grad_wk[...] = whole_a(2, own_2)
    grad_wo[:, 128:256] = whole_b(0)
    grad_wo[:, 0:128] = whole_a(0, own_0)
    grad_wq[:, 0:128] = whole_a(1, own_1)
    grad_wq[:, 128:256] = whole_b(1)
    settle()
    grad_wv[...] = whole_b(2)


def rope_table(count):
    half_head = HEAD_SIZE // 2
    frequencies = np.power(
        np.float32(rope_base), np.float32(-2.0) * np.arange(half_head, dtype=np.float32) / HEAD_SIZE
    ).astype(np.float32)
    angles = np.arange(count, dtype=np.float32)[:, None] * frequencies[None, :]
    return np.concatenate([np.cos(angles), np.sin(angles)], axis=1).astype(np.float32)


def hand_on_kernel(*refs):
    count = len(refs) // 2
    for i in range(count):
        refs[count + i][...] = refs[i][...]


def shards(
    x_prompt,
    x_comp,
    up_prompt,
    up_comp,
    w_q,
    key_projection,
    value_projection,
    w_o,
    pre_gain,
    post_gain,
    dpo_weight,
    prompt_len,
    comp_len,
    loss_mask,
):
    rows_p, rows_c, width = x_prompt.shape[1], x_comp.shape[2], x_prompt.shape[2]
    half, comp = 8 * rows_p, 8 * rows_c
    rope = jnp.asarray(rope_table(2 * half + comp))
    bf, f32 = jnp.bfloat16, jnp.float32
    vm, anywhere, smem = (
        pl.BlockSpec(memory_space=pltpu.VMEM),
        pl.BlockSpec(memory_space=pl.ANY),
        pl.BlockSpec(memory_space=pltpu.SMEM),
    )
    dma = pltpu.SemaphoreType.DMA
    out = pl.pallas_call(
        block_kernel,
        out_shape=(
            jax.ShapeDtypeStruct((rows_p, width), bf),
            jax.ShapeDtypeStruct((rows_c, width), bf),
            jax.ShapeDtypeStruct((144, 256), f32),
            jax.ShapeDtypeStruct((144, 128), f32),
            jax.ShapeDtypeStruct((144, 128), f32),
            jax.ShapeDtypeStruct((144, 256), f32),
        ),
        in_specs=[anywhere] * 8 + [vm] * 2 + [anywhere] + [smem] * 4,
        out_specs=[anywhere] * 2 + [vm] * 4,
        scratch_shapes=[
            pltpu.VMEM((half, 128), f32),
            pltpu.VMEM((half, 128), f32),
            pltpu.VMEM((comp, 128), f32),
            pltpu.VMEM((comp, 128), f32),
            pltpu.VMEM((2 * half + comp, 128), f32),
            pltpu.VMEM((rows_p, width), bf),
            pltpu.VMEM((rows_c, width), bf),
            pltpu.VMEM((rows_p, width), bf),
            pltpu.VMEM((rows_c, width), bf),
            pltpu.VMEM((width, 512), bf),
            pltpu.VMEM((256, width), bf),
            pltpu.VMEM((8, rows_p, width), bf),
            pltpu.VMEM((8, rows_c, width), bf),
            pltpu.VMEM((8, rows_p, width), bf),
            pltpu.VMEM((8, rows_c, width), bf),
            pltpu.VMEM((3 * STEPS, rows_p, PIECE), bf),
            pltpu.VMEM((3 * STEPS, rows_c, PIECE), bf),
            pltpu.VMEM((8, rows_p, width), bf),
            pltpu.VMEM((8, rows_c, width), bf),
            pltpu.VMEM((half + comp, 256), bf),
            pltpu.VMEM((2 * half + comp, 256), bf),
            pltpu.VMEM((half + comp, 256), bf),
            pltpu.VMEM((2, half, 2 * half), f32),
            pltpu.VMEM((2, comp, 2 * half + comp), f32),
            pltpu.VMEM((2, half, 2 * half), f32),
            pltpu.VMEM((2, comp, 2 * half + comp), f32),
            pltpu.VMEM((2 * half, 256), f32),
            pltpu.VMEM((half, 256), bf),
            pltpu.VMEM((half, 256), bf),
            pltpu.VMEM((half + comp, 256), bf),
            pltpu.VMEM((half + comp, 256), bf),
            pltpu.VMEM((3, 2, 2, 8, 2, 144, 128), bf),
            pltpu.VMEM((3, 2, 2, 8, 144, 128), bf),
            pltpu.VMEM((3, 2, 144, 128), bf),
            pltpu.VMEM((3, 2, 3, 2, 144, 128), bf),
            pltpu.VMEM((3, 80, 128), bf),
            pltpu.VMEM((3, 64, 128), bf),
            pltpu.VMEM((3, 2, 3, 144, 128), bf),
            pltpu.VMEM((3, 144, 128), bf),
            pltpu.VMEM((3, 144, 128), bf),
            pltpu.VMEM((3, 8, 144, 128), bf),
            pltpu.VMEM((3, 8, 144, 128), bf),
            pltpu.VMEM((rows_p, width), bf),
            pltpu.VMEM((rows_c, width), bf),
            dma((9,)),
            dma((6,)),
            dma((18 * STEPS,)),
            dma((2,)),
            dma((2,)),
            dma((12,)),
            dma((12,)),
            dma((48,)),
            dma((48,)),
            dma((3,)),
            dma((3,)),
            dma((6,)),
            dma((6,)),
            dma((2,)),
        ],
        compiler_params=pltpu.CompilerParams(
            collective_id=1, has_side_effects=True, vmem_limit_bytes=60 << 20
        ),
        name="block",
    )(
        x_prompt[0], x_comp[0, 0], up_prompt[0], up_comp[0, 0],
        w_q, key_projection, value_projection, w_o,
        pre_gain, post_gain, rope,
        dpo_weight, prompt_len, comp_len, loss_mask[0, 0],
    )
    out_p, out_c, grad_wq, grad_wk, grad_wv, grad_wo = pl.pallas_call(
        hand_on_kernel,
        out_shape=tuple(jax.ShapeDtypeStruct(o.shape, o.dtype) for o in out),
        in_specs=[vm] * 6,
        out_specs=[vm] * 6,
        name="hand_on",
    )(*out)
    return (out_p[None], out_c[None, None], grad_wq, grad_wk, grad_wv, grad_wo.T)


def solution(mesh):
    in_specs = (
        P("dp", ("pair", "tp"), None),
        P("dp", "pair", "tp", None),
        P("dp", ("pair", "tp"), None),
        P("dp", "pair", "tp", None),
        P(None, "tp"),
        P(None, "tp"),
        P(None, "tp"),
        P("tp", None),
        P(),
        P(),
        P("dp"),
        P("dp"),
        P("dp", "pair"),
        P("dp", "pair", None),
    )
    out_specs = (
        P("dp", ("pair", "tp"), None),
        P("dp", "pair", "tp", None),
        P(("pair", "dp"), "tp"),
        P(("pair", "dp"), "tp"),
        P(("pair", "dp"), "tp"),
        P("tp", ("pair", "dp")),
    )
    return jax.shard_map(shards, mesh=mesh, in_specs=in_specs, out_specs=out_specs, check_vma=False)
```
